256 devices in a mesh: dp: 64 (over x, z, core), fsdp: 4 (over y).
Axes of the slice: x: 4, y: 4, z: 8, core: 2. Of those that a mesh axis runs over, the one named last changes fastest.
Arguments:
- item_states: bfloat16 [256, 256, 4096], P('dp', None, 'fsdp'), may hold values from -6 to 6
- item_scores: float32 [256, 16, 256], P('dp'), may hold values from -8 to 8
- item_lengths: int32 [256], P('dp'), may hold values from 1 to 256, 32768 in all
- item_gain: float32 [4096], P('fsdp'), may hold values from 0.25 to 1.75
- value_weight: bfloat16 [4096, 2048], P('fsdp'), may hold values from -0.09375 to 0.09375
- user_items: int32 [64, 1024], P('dp', 'fsdp'), may hold values from 0 to 255
- negatives: int32 [64, 256], P('dp'), may hold values from 0 to 255
- position_embed: bfloat16 [1024, 2048], P('fsdp'), may hold values from -3 to 3
- user_gain: float32 [2048], replicated, may hold values from 0.25 to 1.75
- user_weight: bfloat16 [2048, 2048], P('fsdp'), may hold values from -0.125 to 0.125
Outputs:
- item_grads: float32 [256, 2048], P('dp')
- weight_grad: bfloat16 [2048, 2048], P('fsdp')
The draws below stay inside these ranges and needn't reach their ends.
Inputs may be any that keep to these rules, and one draw needn't show every extreme that they name: `user_items`: item ids of the catalogue. `negatives`: item ids of the catalogue. `item_lengths`: one or more tokens of each text are used.
All inputs are finite; a program needn't handle non-finite values. No bound on the sum of `item_lengths` on one device may be relied on, other than what follows from the above.
Results may differ from the reference program's by a relative error of at most 0.022.
Values may be sent and summed in bfloat16 or wider, within the bound.
A program may use at most 128 MiB of HBM per device.

```python
import math
import jax
import jax.numpy as jnp
import numpy as np
from jax import lax

D = 4096
HEADS = 16
HEAD = 128
LTXT = 256
ULEN = 1024
NEG = 256
HV = 2048
ITEMS = 256
USERS = 64


def place_ends(entries, key, low, top_value):
    longest = entries.shape.index(max(entries.shape))
    spots = []
    for shift in (0, 1):
        where = [jax.random.randint(jax.random.fold_in(key, axis), (), 0, length) for axis, length in enumerate(entries.shape)]
        where[longest] = (where[longest] + shift) % entries.shape[longest]
        spots.append(tuple(where))
    return entries.at[spots[0]].set(low).at[spots[1]].set(top_value)


def steps_of(own_key, dims, split, low, high):
    factor_of, own = 1.0, jax.random.fold_in(own_key, 6)
    for dim, shards_of in split:
        heights = jnp.exp(jax.random.uniform(jax.random.fold_in(own, dim), (shards_of,), jnp.float32, low / len(split), high / len(split)))
        factor_of = factor_of * jnp.repeat(heights, dims[dim] // shards_of).reshape([-1 if axis == dim else 1 for axis in range(len(dims))])
    return factor_of


def cumulative_ranks(count, slope):
    loads = [(1 << 20) // math.isqrt(standing ** slope) + 1 for standing in range(1, count + 1)]
    spread = 1 + sum(loads) // (1 << 30)
    return np.cumsum(np.array([max(1, weight // spread) for weight in loads]))


def skewed_ids(own_key, extent, amount, slope):
    listing = cumulative_ranks(amount, slope)
    pick = jax.random.randint(jax.random.fold_in(own_key, 1), extent, 0, int(listing[amount - 1]))
    standing = jnp.searchsorted(jnp.asarray(listing, jnp.int32), pick, side="right")
    return jax.random.permutation(jax.random.fold_in(own_key, 2), amount)[standing].astype(jnp.int32)


def split_up(count, total, most, lean):
    portions = [(1 << 20) // math.isqrt(standing ** lean) + 1 for standing in range(2, count + 1)]
    surplus, counts = total - most - (count - 1), [1] * (count - 1)
    while surplus > 0:
        free = [i for i in range(count - 1) if counts[i] < most]
        whole, budget = sum([portions[i] for i in free]), surplus
        for i in free:
            extra = min(most - counts[i], max(1, budget * portions[i] // whole), surplus)
            counts[i] = counts[i] + extra
            surplus = surplus - extra
    return np.array([most] + counts)


def ragged_sizes(stream_key, amount, total, reach, lean):
    if amount == 2:
        one = jax.random.randint(stream_key, (), max(1, total - reach), min(reach, total - 1) + 1)
        return jnp.stack([one, total - one])
    lengths = jnp.asarray(split_up(amount, total, reach, lean), jnp.int32)
    couples = (amount - 1) // 2
    source_of, receiver = lengths[1:1 + 2 * couples:2], lengths[2:2 + 2 * couples:2]
    room = jnp.minimum(source_of - 1, reach - receiver)
    passed = jax.random.randint(jax.random.fold_in(stream_key, 1), (couples,), 0, 1 << 20) % (room + 1)
    lengths = lengths.at[1:1 + 2 * couples:2].set(source_of - passed).at[2:2 + 2 * couples:2].set(receiver + passed)
    return lengths[jax.random.permutation(jax.random.fold_in(stream_key, 2), amount)]


def normal_values(rng, shape, deviation, reach, cuts=(), held_as=jnp.bfloat16):
    values = jax.random.normal(rng, shape, jnp.float32) * deviation
    if len(cuts) > 0:
        values = steps_of(rng, shape, cuts, -0.22, 0.18) * values
    return jnp.clip(values, min=-reach, max=reach).astype(held_as)


def setup_inputs(seed: int = 0) -> dict:
    key_list = jax.random.split(jax.random.key(seed), 11)
    item_states = normal_values(key_list[0], (ITEMS, LTXT, D), 1.0, 6.0, ((0, 64), (2, 4)))
    item_scores = normal_values(key_list[1], (ITEMS, HEADS, LTXT), 2.0, 8.0, ((0, 64),), jnp.float32)
    item_lengths = ragged_sizes(key_list[2], ITEMS, ITEMS * LTXT // 2, LTXT, 2).astype(jnp.int32)
    item_gain = jnp.clip(1.0 + 0.15 * jax.random.normal(key_list[3], (D,), jnp.float32), 0.25, 1.75)
    value_weight = normal_values(key_list[4], (D, HV), D ** -0.5, 0.09375, ((0, 4),))
    user_items = place_ends(skewed_ids(key_list[5], (USERS, ULEN), ITEMS, 2), jax.random.fold_in(key_list[5], 3), 0, ITEMS - 1).astype(jnp.int32)
    negatives = place_ends(jax.random.randint(key_list[6], (USERS, NEG), 0, ITEMS), jax.random.fold_in(key_list[6], 1), 0, ITEMS - 1).astype(jnp.int32)
    position_embed = normal_values(key_list[7], (ULEN, HV), 0.3, 3.0, ((0, 4),))
    user_gain = jnp.clip(1.0 + 0.15 * jax.random.normal(key_list[8], (HV,), jnp.float32), 0.25, 1.75)
    user_weight = normal_values(key_list[9], (HV, HV), HV ** -0.5, 0.125, ((0, 4),))
    return {"item_states": item_states, "item_scores": item_scores, "item_lengths": item_lengths, "item_gain": item_gain, "value_weight": value_weight, "user_items": user_items, "negatives": negatives, "position_embed": position_embed, "user_gain": user_gain, "user_weight": user_weight}


def unit_rows(vectors):
    length = jnp.sqrt(lax.optimization_barrier(jnp.sum(vectors * vectors, axis=1, keepdims=True)) + 1e-06)
    return (vectors / length, length)

def reference(item_states, item_scores, item_lengths, item_gain, value_weight, user_items, negatives, position_embed, user_gain, user_weight):
    position = jnp.arange(LTXT)

    def encode(pieces):
        states, scores, length = pieces
        states_f = states.astype(jnp.float32)
        inv_rms = lax.rsqrt(lax.optimization_barrier(jnp.mean(states_f * states_f, axis=1)) + 1e-05)
        scaled = (states_f * item_gain).astype(jnp.bfloat16)
        values = jnp.dot(scaled, value_weight, preferred_element_type=jnp.float32).reshape(LTXT, HEADS, HEAD)
        weights = jnp.where(position[None, :] < length, jnp.exp(scores), 0.0)
        numerator = jnp.einsum('ht,thc->hc', weights * inv_rms[None, :], values)
        totals = lax.optimization_barrier(jnp.sum(weights, axis=1))
        return (numerator / totals[:, None]).reshape(HV).astype(jnp.bfloat16)
    item_embed = lax.map(encode, (item_states, item_scores, item_lengths))
    scale_loss = 1.0 / (USERS * (ULEN - 1))
    valid_rows = (jnp.arange(ULEN) < ULEN - 1).astype(jnp.float32)
    highest = lax.Precision.HIGHEST
    place_f = position_embed.astype(jnp.float32)

    def per_user(carry, pieces):
        weight_acc, grad_acc = carry
        item_ids, neg_ids = pieces
        rows_f = jnp.take(item_embed, item_ids, axis=0).astype(jnp.float32)
        input_f = rows_f + place_f
        inv_user = lax.rsqrt(lax.optimization_barrier(jnp.mean(input_f * input_f, axis=1, keepdims=True)) + 1e-05)
        user_normed = (input_f * inv_user * user_gain).astype(jnp.bfloat16)
        output = input_f + jnp.dot(user_normed, user_weight, preferred_element_type=jnp.float32)
        target = jnp.concatenate([rows_f[1:], jnp.zeros((1, HV), jnp.float32)], axis=0)
        neg_rows = jnp.take(item_embed, neg_ids, axis=0).astype(jnp.float32)
        out_unit, out_len = unit_rows(output)
        tgt_unit, tgt_len = unit_rows(target)
        neg_unit, neg_len = unit_rows(neg_rows)
        pos_logit = 20.0 * lax.optimization_barrier(jnp.sum(out_unit * tgt_unit, axis=1))
        neg_logit = 20.0 * jnp.dot(out_unit, neg_unit.T, precision=highest)
        log_total = jnp.log(jnp.exp(pos_logit) + lax.optimization_barrier(jnp.sum(jnp.exp(neg_logit), axis=1)))
        pos_grad = scale_loss * valid_rows * (jnp.exp(pos_logit - log_total) - 1.0)
        neg_grad = scale_loss * valid_rows[:, None] * jnp.exp(neg_logit - log_total[:, None])
        out_unit_grad = 20.0 * (pos_grad[:, None] * tgt_unit + jnp.dot(neg_grad, neg_unit, precision=highest))
        tgt_unit_grad = 20.0 * pos_grad[:, None] * out_unit
        neg_unit_grad = 20.0 * jnp.dot(neg_grad.T, out_unit, precision=highest)
        grad_out = (out_unit_grad - out_unit * lax.optimization_barrier(jnp.sum(out_unit * out_unit_grad, axis=1, keepdims=True))) / out_len
        tgt_grad = (tgt_unit_grad - tgt_unit * lax.optimization_barrier(jnp.sum(tgt_unit * tgt_unit_grad, axis=1, keepdims=True))) / tgt_len
        neg_row_grad = (neg_unit_grad - neg_unit * lax.optimization_barrier(jnp.sum(neg_unit * neg_unit_grad, axis=1, keepdims=True))) / neg_len
        grad_cast = grad_out.astype(jnp.bfloat16)
        weight_acc = weight_acc + jnp.dot(user_normed.T, grad_cast, preferred_element_type=jnp.float32)
        normed_grad = jnp.dot(grad_cast, user_weight.T, preferred_element_type=jnp.float32)
        gained = user_gain * normed_grad
        grad_rows = grad_out + inv_user * gained - input_f * inv_user ** 3 * lax.optimization_barrier(jnp.mean(gained * input_f, axis=1, keepdims=True))
        grad_rows = grad_rows + jnp.concatenate([jnp.zeros((1, HV), jnp.float32), tgt_grad[:-1]], axis=0)
        row_cast = grad_rows.astype(jnp.bfloat16).astype(jnp.float32)
        grad_acc = grad_acc + jax.ops.segment_sum(row_cast, item_ids, num_segments=ITEMS)
        grad_acc = grad_acc + jax.ops.segment_sum(neg_row_grad, neg_ids, num_segments=ITEMS)
        return ((weight_acc, grad_acc), None)
    start = (jnp.zeros((HV, HV), jnp.float32), jnp.zeros((ITEMS, HV), jnp.float32))
    final, unused = lax.scan(per_user, start, (user_items, negatives))
    weight_acc, grad_acc = final
    return (grad_acc, weight_acc.astype(jnp.bfloat16))
```

```python
import jax
import jax.numpy as jnp
from jax import lax
from jax.experimental import pallas as pl
from jax.experimental.pallas import tpu as pltpu
from jax.sharding import PartitionSpec as P

MESH = pl.DeviceIdType.MESH
F32, BF16 = jnp.float32, jnp.bfloat16
NX, NY, NZ = 4, 4, 8
D, HV, ULEN, USERS = 4096, 2048, 1024, 64
VM = pl.BlockSpec(memory_space=pltpu.VMEM)
ANY = pl.BlockSpec(memory_space=pl.ANY)


def place():
    d, y = lax.axis_index("dp"), lax.axis_index("fsdp")
    return lax.div(d, 16), y, lax.rem(lax.div(d, 2), 8), lax.rem(d, 2)


def ring(i, o, n):
    return lax.rem(i + o + n, n)


def at128(i):
    return pl.multiple_of(i, 128)


def at16(i):
    return pl.multiple_of(i, 16)


def nt(a, b):
    return lax.dot_general(a, b, (((1,), (1,)), ((), ())), preferred_element_type=F32)


def tn(a, b):
    return lax.dot_general(a, b, (((0,), (0,)), ((), ())), preferred_element_type=F32)


def mm(a, b):
    return jnp.dot(a, b, preferred_element_type=F32)


def split(v):
    hi = v.astype(BF16)
    return hi, (v - hi.astype(F32)).astype(BF16)


def meet(peers):
    barrier = pltpu.get_barrier_semaphore()
    for x, y, z, c in peers:
        pl.semaphore_signal(barrier, inc=1, device_id=((x * NZ + z) * 2 + c, y), device_id_type=MESH)
    pl.semaphore_wait(barrier, len(peers))


class Net:
    def __init__(self, send, recv):
        self.send, self.recv, self.all = send, recv, []

    def put(self, src, dst, where):
        x, y, z, c = where
        k = len(self.all)
        copy = pltpu.make_async_remote_copy(
            src_ref=src,
            dst_ref=dst,
            send_sem=self.send.at[k],
            recv_sem=self.recv.at[k],
            device_id=((x * NZ + z) * 2 + c, y),
            device_id_type=MESH,
        )
        copy.start()
        self.all.append(copy)
        return copy

    def drain(self):
        for copy in self.all:
            copy.wait_send()


def landed(copies):
    for copy in copies:
        copy.wait_recv()


A_COPIES = 104


def items_kernel(
    lengths, states_h, scores, igain, vweight_h, pos_h, ugain, uweight_h, ids,
    ce, pp, posx, nxt,
    states, vweight, uweight, squares, squares_in, num, num_in, cat, ep, ep_in, pin, pback, pback_in,
    send, recv, local,
):
    x, y, z, c = place()
    low = lax.rem(z, 2)
    group = 4 * x + lax.div(z, 2)
    member, quarter = 2 * low + c, 2 * c + low
    base = z - low
    net = Net(send, recv)

    def peer(dx=0, dy=0, dz=0, dc=0):
        return ring(x, dx, NX), ring(y, dy, NY), ring(z, dz, NZ), ring(c, dc, 2)

    def mate(om, oy):
        m = ring(member, om, 4)
        return x, ring(y, oy, NY), base + lax.div(m, 2), lax.rem(m, 2)

    loads = [
        pltpu.make_async_copy(states_h, states, local.at[0]),
        pltpu.make_async_copy(uweight_h, uweight, local.at[1]),
        pltpu.make_async_copy(vweight_h, vweight, local.at[2]),
        pltpu.make_async_copy(
            pos_h.at[pl.ds(at16(16 * group), 16), pl.ds(at128(512 * y), 512)], pin.at[0], local.at[3]
        ),
        pltpu.make_async_copy(pos_h.at[:, pl.ds(at128(512 * y + 128 * x), 128)], posx.at[y], local.at[4]),
    ]
    for load in loads:
        load.start()
    offsets = [(om, oy) for om in range(4) for oy in range(4) if om or oy]
    meet(
        [mate(om, oy) for om, oy in offsets]
        + [peer(dz=o) for o in range(1, NZ)]
        + [peer(dx=o) for o in range(1, NX)]
    )

    rows16 = pl.ds(at16(16 * group), 16)
    pin_copies, posx_copies = [], []
    for o in range(1, NY):
        to = ring(y, o, NY)
        pin_copies.append(net.put(pos_h.at[rows16, pl.ds(at128(512 * to), 512)], pin.at[o], peer(dy=o)))
    next_copy = net.put(ids, nxt, peer(dy=-1))
    for o in range(1, NY):
        to = ring(y, o, NY)
        posx_copies.append(
            net.put(pos_h.at[:, pl.ds(at128(512 * to + 128 * x), 128)], posx.at[y], peer(dy=o))
        )

    loads[0].wait()
    ones = jnp.ones((8, 128), F32)
    item_row = lax.broadcasted_iota(jnp.int32, (8, 256), 0)
    sums = jnp.zeros((8, 256), F32)
    for i in range(4):
        part = jnp.zeros((256, 128), F32)
        for j in range(8):
            v = states[i, :, 128 * j:128 * (j + 1)].astype(F32)
            part = part + v * v
        hi, lo = split(part)
        low2 = (part - hi.astype(F32) - lo.astype(F32)).astype(BF16)
        ones16 = ones.astype(BF16)
        sums = jnp.where(item_row == i, nt(ones16, hi) + nt(ones16, lo) + nt(ones16, low2), sums)
    squares[...] = sums
    square_copies = [net.put(squares, squares_in.at[o - 1], peer(dy=o)) for o in range(1, NY)]

    loads[1].wait()
    loads[3].wait()
    landed(pin_copies)
    gain_part = ugain[:, pl.ds(at128(512 * y), 512)]
    pos_rows = pin[...].astype(F32).reshape(64, 512) * gain_part
    pback[...] = mm(
        pos_rows.astype(BF16), uweight[:, pl.ds(at128(512 * quarter), 512)]
    ).reshape(4, 16, 512)
    back_copies = [net.put(pback.at[o], pback_in.at[o - 1], peer(dy=-o)) for o in range(1, NY)]

    landed(square_copies)
    inv_rms = lax.rsqrt((squares[...] + squares_in[0] + squares_in[1] + squares_in[2]) / D + 1e-05)
    token = lax.broadcasted_iota(jnp.int32, (16, 256), 1)
    pooled_hi, pooled_lo = [], []
    for i in range(4):
        weights = jnp.where(token < lengths[i], jnp.exp(scores[i]), 0.0)
        weights = weights * (inv_rms[i:i + 1] / jnp.sum(weights, axis=1, keepdims=True))
        hi, lo = split(weights)
        both = mm(jnp.concatenate([hi, lo], axis=0), states[i])
        pooled = (both[:16] + both[16:]) * igain[...]
        hi, lo = split(pooled)
        pooled_hi.append(hi)
        pooled_lo.append(lo)
    left = jnp.concatenate(pooled_hi + pooled_lo, axis=0)
    loads[2].wait()
    head = lax.broadcasted_iota(jnp.int32, (4, 16, 256), 1)
    tile = lax.broadcasted_iota(jnp.int32, (4, 16, 256), 2) // 128
    for j in range(8):
        full = mm(left, vweight[:, 256 * j:256 * (j + 1)])
        full = (full[:64] + full[64:]).reshape(4, 16, 256)
        block = jnp.sum(jnp.where(head == tile + 2 * j, full, 0.0), axis=1)
        num[j // 2, 4 * (j % 2):4 * (j % 2) + 4, :] = block
    num_copies = []
    for om, oy in offsets:
        num_copies.append(net.put(num.at[ring(y, oy, NY)], num_in.at[oy, member], mate(om, oy)))
    num_in[0, pl.ds(member, 1)] = num[pl.ds(y, 1)]

    landed(back_copies)
    pp_rows, pp_cols = rows16, pl.ds(at128(512 * quarter), 512)
    pp[pp_rows, pp_cols] = (pback[0] + pback_in[0] + pback_in[1] + pback_in[2]).astype(BF16)
    own = pp.at[pp_rows, pp_cols]
    pp_z = [net.put(own, own, peer(dz=o)) for o in range(1, NZ)]

    landed(num_copies)
    for m in range(4):
        total = num_in[0, m] + num_in[1, m] + num_in[2, m] + num_in[3, m]
        cat[4 * m:4 * m + 4, :256] = total[:4]
        cat[4 * m:4 * m + 4, 256:] = total[4:]
    embed = cat[...].astype(BF16)
    gained = (embed.astype(F32) * gain_part).astype(BF16)
    for t in range(NY):
        ep[t] = mm(gained, uweight[:, pl.ds(at128(512 * t + 128 * quarter), 128)])
    ep_copies = [net.put(ep.at[ring(y, o, NY)], ep_in.at[o - 1], peer(dy=o)) for o in range(1, NY)]
    ce_cols = pl.ds(at128(512 * y + 128 * quarter), 128)
    ce[0, rows16, ce_cols] = cat[:, pl.ds(at128(128 * quarter), 128)].astype(BF16)
    block = ce.at[0, rows16, ce_cols]
    cat_z = [net.put(block, block, peer(dz=o)) for o in range(1, NZ)]

    landed(pp_z)
    own = pp.at[pl.ds(at16(64 * x), 64), pl.ds(at128(1024 * c), 1024)]
    pp_x = [net.put(own, own, peer(dx=o)) for o in range(1, NX)]

    landed(ep_copies)
    ce[1, rows16, ce_cols] = (ep[pl.ds(y, 1)][0] + ep_in[0] + ep_in[1] + ep_in[2]).astype(BF16)
    block = ce.at[1, rows16, ce_cols]
    ep_z = [net.put(block, block, peer(dz=o)) for o in range(1, NZ)]

    rows64 = pl.ds(at16(64 * x), 64)

    def cols(t):
        return pl.ds(at128(512 * t + 256 * c), 256)

    landed(cat_z)
    block = ce.at[0, rows64, cols(y)]
    cat_x = [net.put(block, block, peer(dx=o)) for o in range(1, NX)]
    landed(ep_z)
    block = ce.at[1, rows64, cols(y)]
    ep_y = [net.put(block, block, peer(dy=o)) for o in range(1, NY)]

    landed(pp_x)
    own = pp.at[:, pl.ds(at128(1024 * c), 1024)]
    final = [net.put(own, own, peer(dc=1))]

    landed(cat_x)
    block = ce.at[0, :, cols(y)]
    cat_y = [net.put(block, block, peer(dy=o)) for o in range(1, NY)]
    final.append(net.put(block, block, peer(dc=1)))
    landed(ep_y)
    ep_x = []
    for o in range(1, NX):
        for t in range(NY):
            block = ce.at[1, rows64, cols(t)]
            ep_x.append(net.put(block, block, peer(dx=o)))
    for t in range(NY):
        block = ce.at[1, rows64, cols(t)]
        final.append(net.put(block, block, peer(dc=1)))
    for o in range(1, NY):
        cat_y[o - 1].wait_recv()
        block = ce.at[0, :, cols(ring(y, -o, NY))]
        final.append(net.put(block, block, peer(dc=1)))
    for o in range(1, NX):
        landed(ep_x[4 * (o - 1):4 * o])
        for t in range(NY):
            block = ce.at[1, pl.ds(at16(64 * ring(x, -o, NX)), 64), cols(t)]
            final.append(net.put(block, block, peer(dc=1)))
    landed(final)
    landed(posx_copies)
    landed([next_copy])
    loads[4].wait()
    net.drain()


def items(lengths, states, scores, igain, vweight, pos, ugain, uweight, ids):
    return pl.pallas_call(
        items_kernel,
        out_shape=(
            jax.ShapeDtypeStruct((2, 256, HV), BF16),
            jax.ShapeDtypeStruct((256, HV), BF16),
            jax.ShapeDtypeStruct((4, 256, 128), BF16),
            jax.ShapeDtypeStruct((8, 256), jnp.int32),
        ),
        in_specs=[pl.BlockSpec(memory_space=pltpu.SMEM), ANY, VM, VM, ANY, ANY, VM, ANY, VM],
        out_specs=(VM, VM, VM, VM),
        scratch_shapes=[
            pltpu.VMEM((4, 256, 1024), BF16),
            pltpu.VMEM((1024, HV), BF16),
            pltpu.VMEM((512, HV), BF16),
            pltpu.VMEM((8, 256), F32),
            pltpu.VMEM((3, 8, 256), F32),
            pltpu.VMEM((4, 8, 256), F32),
            pltpu.VMEM((4, 4, 8, 256), F32),
            pltpu.VMEM((16, 512), F32),
            pltpu.VMEM((4, 16, 128), F32),
            pltpu.VMEM((3, 16, 128), F32),
            pltpu.VMEM((4, 16, 512), BF16),
            pltpu.VMEM((4, 16, 512), F32),
            pltpu.VMEM((3, 16, 512), F32),
            pltpu.SemaphoreType.DMA((A_COPIES,)),
            pltpu.SemaphoreType.DMA((A_COPIES,)),
            pltpu.SemaphoreType.DMA((5,)),
        ],
        compiler_params=pltpu.CompilerParams(
            collective_id=0, has_side_effects=True, vmem_limit_bytes=40 * 2**20
        ),
        name="items",
    )(lengths, states, scores, igain, vweight, pos, ugain, uweight, ids)


CHUNK = 512


def users_kernel(
    ids, targets, negs, valid, ce, pp, pos,
    s_out, q_out, r_out,
    in_v, ep_v, u_v, uh_v, ug_v, iu_v,
):
    js = [slice(j, j + CHUNK) for j in range(0, HV, CHUNK)]
    item = lax.broadcasted_iota(jnp.int32, (256, 256), 0)
    hot_t32 = (item == ids[...]).astype(F32)
    hot_t = hot_t32.astype(BF16)
    hot = hot_t32.T.astype(BF16)
    target_t = (item == targets[...]).astype(F32)
    counts = jnp.sum((item == negs[...]).astype(F32), axis=1, keepdims=True)

    squares = jnp.zeros((256, 1), F32)
    cat_squares = jnp.zeros((256, 1), F32)
    for j in js:
        v = mm(hot, ce[0, :, j]) + pos[:, j].astype(F32)
        in_v[:, j] = v
        squares += jnp.sum(v * v, axis=1, keepdims=True)
        w = ce[0, :, j].astype(F32)
        cat_squares += jnp.sum(w * w, axis=1, keepdims=True)
    inv = lax.rsqrt(squares / HV + 1e-05)
    cat_inv = 1.0 / jnp.sqrt(cat_squares + 1e-06)
    out_squares = jnp.zeros((256, 1), F32)
    for j in js:
        e = mm(hot, ce[1, :, j]) + pp[:, j].astype(F32)
        ep_v[:, j] = e
        v = in_v[:, j] + inv * e
        u_v[:, j] = v
        out_squares += jnp.sum(v * v, axis=1, keepdims=True)
    out_inv = 1.0 / jnp.sqrt(out_squares + 1e-06)
    logits = jnp.zeros((256, 256), F32)
    for j in js:
        u = u_v[:, j] * out_inv
        u_v[:, j] = u
        hi, lo = split(u)
        uh_v[:, j] = hi
        logits += nt(ce[0, :, j], hi) + nt(ce[0, :, j], lo)
    powers = jnp.exp(20.0 * cat_inv * logits)
    pos_power = jnp.sum(target_t * powers, axis=0, keepdims=True)
    total = pos_power + jnp.sum(counts * powers, axis=0, keepdims=True)
    scale = valid[...] * (1.0 / (USERS * (ULEN - 1)))
    grad_t = scale * (counts * powers / total + target_t * (pos_power / total - 1.0))
    by_item = grad_t.astype(BF16)
    by_row_hi, by_row_lo = split((grad_t * cat_inv).T)
    along = jnp.zeros((256, 1), F32)
    cat_along = jnp.zeros((256, 1), F32)
    for j in js:
        v = 20.0 * (mm(by_row_hi, ce[0, :, j]) + mm(by_row_lo, ce[0, :, j]))
        ug_v[:, j] = v
        along += jnp.sum(v * u_v[:, j], axis=1, keepdims=True)
        v = 20.0 * mm(by_item, uh_v[:, j])
        iu_v[:, j] = v
        cat_along += jnp.sum(v * ce[0, :, j].astype(F32), axis=1, keepdims=True)
    cat_along = cat_along * cat_inv * cat_inv
    inner = jnp.zeros((256, 1), F32)
    for j in js:
        g = (ug_v[:, j] - u_v[:, j] * along) * out_inv
        ug_v[:, j] = g
        inner += jnp.sum(g * ep_v[:, j], axis=1, keepdims=True)
    inner = inner * (inv * inv * inv / HV)
    for j in js:
        g = ug_v[:, j]
        q = (inv * g).astype(BF16)
        q_out[:, j] = q
        s_out[:, j] = mm(hot_t, q).astype(BF16)
        direct = (g - in_v[:, j] * inner).astype(BF16)
        item_grad = (iu_v[:, j] - ce[0, :, j].astype(F32) * cat_along) * cat_inv
        r_out[:, j] = (mm(hot_t, direct) + item_grad).astype(BF16)


def users(ids, targets, negs, valid, ce, pp, pos):
    shape = jax.ShapeDtypeStruct((256, HV), BF16)
    return pl.pallas_call(
        users_kernel,
        out_shape=(shape, shape, shape),
        in_specs=[VM] * 7,
        out_specs=(VM, VM, VM),
        scratch_shapes=[
            pltpu.VMEM((256, HV), F32),
            pltpu.VMEM((256, HV), F32),
            pltpu.VMEM((256, HV), F32),
            pltpu.VMEM((256, HV), BF16),
            pltpu.VMEM((256, HV), F32),
            pltpu.VMEM((256, HV), F32),
        ],
        compiler_params=pltpu.CompilerParams(vmem_limit_bytes=48 * 2**20),
        name="users",
    )(ids, targets, negs, valid, ce, pp, pos)


C_COPIES = 100


def grads_kernel(
    s, q, r, ce_h, posx, ugain, uweight_h,
    item_out, weight_out,
    cat, uweight,
    s1_in, q1_in, r1_in, s1, q1, r1,
    s2_in, r2_in, q2_in, s2, r2, q2,
    s3_in, r3_in, q3_in, s3, r3,
    s4_in, qg, sg, t, t_in, item,
    send, recv, local,
):
    x, y, z, c = place()
    net = Net(send, recv)

    def peer(dx=0, dy=0, dz=0, dc=0):
        return ring(x, dx, NX), ring(y, dy, NY), ring(z, dz, NZ), ring(c, dc, 2)

    zc = [(dz, dc) for dc in range(2) for dz in range(NZ) if dz or dc]
    xy = [(dx, dy) for dx in range(NX) for dy in range(NY) if dx or dy]
    loads = [
        pltpu.make_async_copy(ce_h.at[0, :, pl.ds(at128(512 * y + 128 * x), 128)], cat, local.at[0]),
        pltpu.make_async_copy(uweight_h.at[:, pl.ds(at128(1024 * c + 128 * z), 128)], uweight, local.at[1]),
    ]
    for load in loads:
        load.start()
    meet([peer(dz=dz, dc=dc) for dz, dc in zc] + [peer(dx=dx, dy=dy) for dx, dy in xy])

    mine = pl.ds(at128(1024 * c), 1024)
    theirs = pl.ds(at128(1024 * ring(c, 1, 2)), 1024)
    s_copy = net.put(s.at[:, theirs], s1_in, peer(dc=1))
    r_copy = net.put(r.at[:, ring(c, 1, 2)], r1_in, peer(dc=1))
    q_copy = net.put(q.at[:, theirs], q1_in, peer(dc=1))
    s_copy.wait_recv()
    s1[...] = (s[:, mine].astype(F32) + s1_in[...].astype(F32)).astype(BF16)
    s2_copies = [
        net.put(s1.at[pl.ds(at16(64 * ring(y, o, NY)), 64)], s2_in.at[o - 1], peer(dy=o)) for o in range(1, NY)
    ]
    r_copy.wait_recv()
    r1[...] = (r[:, pl.ds(c, 1)].reshape(4, 32, HV).astype(F32) + r1_in[...].astype(F32)).astype(BF16)
    r2_copies = [
        net.put(r1.at[:, :, pl.ds(at128(512 * ring(y, o, NY)), 512)], r2_in.at[o - 1], peer(dy=o))
        for o in range(1, NY)
    ]
    q_copy.wait_recv()
    q1[...] = (q[:, mine].astype(F32) + q1_in[...].astype(F32)).astype(BF16)
    q2_copies = [
        net.put(q1.at[pl.ds(at16(64 * ring(x, o, NX)), 64)], q2_in.at[o - 1], peer(dx=o)) for o in range(1, NX)
    ]

    def added(own, parts):
        total = own.astype(F32)
        for k in range(3):
            total = total + parts[k].astype(F32)
        return total

    landed(s2_copies)
    s2[...] = added(s1[pl.ds(at16(64 * y), 64)], s2_in).astype(BF16)
    s3_copies = [
        net.put(s2.at[pl.ds(at16(16 * ring(x, o, NX)), 16)], s3_in.at[o - 1], peer(dx=o)) for o in range(1, NX)
    ]
    landed(q2_copies)
    q2[...] = added(q1[pl.ds(at16(64 * x), 64)], q2_in).astype(BF16)
    q3_copies = [
        net.put(q2.at[:, pl.ds(at128(128 * ring(z, o, NZ)), 128)], q3_in.at[o - 1], peer(dz=o))
        for o in range(1, NZ)
    ]
    landed(r2_copies)
    r2[...] = added(r1[:, :, pl.ds(at128(512 * y), 512)], r2_in).astype(BF16)
    r3_copies = [net.put(r2.at[ring(x, o, NX)], r3_in.at[o - 1], peer(dx=o)) for o in range(1, NX)]

    landed(s3_copies)
    s3[...] = added(s2[pl.ds(at16(16 * x), 16)], s3_in).astype(BF16)
    s4_copies = [
        net.put(s3.at[:, pl.ds(at128(128 * ring(z, o, NZ)), 128)], s4_in.at[o - 1], peer(dz=o))
        for o in range(1, NZ)
    ]
    landed(q3_copies)
    total = q2[:, pl.ds(at128(128 * z), 128)].astype(F32)
    for k in range(NZ - 1):
        total = total + q3_in[k].astype(F32)
    spot = 4 * y + x
    qg[pl.ds(spot, 1)] = total.astype(BF16)[None]
    qg_copies = [net.put(qg.at[spot], qg.at[spot], peer(dx=dx, dy=dy)) for dx, dy in xy]
    landed(s4_copies)
    total = s3[:, pl.ds(at128(128 * z), 128)].astype(F32)
    for k in range(NZ - 1):
        total = total + s4_in[k].astype(F32)
    sg[pl.ds(spot, 1)] = total.astype(BF16)[None]
    sg_copies = [net.put(sg.at[spot], sg.at[spot], peer(dx=dx, dy=dy)) for dx, dy in xy]
    landed(r3_copies)
    r3[...] = added(r2[pl.ds(x, 1)][0], r3_in)

    for load in loads:
        load.wait()
    gain_rows = ugain[:, pl.ds(at128(512 * y + 128 * x), 128)]
    landed(qg_copies)
    positions = (posx[...].astype(F32).reshape(1024, 128) * gain_rows).astype(BF16)
    tile = tn(positions, qg[...].reshape(1024, 128))
    landed(sg_copies)
    embeds = (cat[...].astype(F32) * gain_rows).astype(BF16)
    tile = tile + tn(embeds, sg[...].reshape(256, 128))
    wrows = pl.ds(at16(128 * x), 128)
    wcols = pl.ds(at128(1024 * c + 128 * z), 128)
    weight_out[wrows, wcols] = tile.astype(BF16)
    block = weight_out.at[wrows, wcols]
    weight_z = [net.put(block, block, peer(dz=o)) for o in range(1, NZ)]

    back = nt(sg[pl.ds(4 * x, 4)].reshape(64, 128), uweight[...]) * ugain[:, pl.ds(at128(512 * y), 512)]
    half = lax.broadcasted_iota(jnp.int32, (64, 512), 0) // 32
    both = jnp.concatenate([r3[...], r3[...]], axis=0)
    back = back + jnp.where(half == c, both, 0.0)
    back = back.reshape(16, 4, 512)
    t[...] = jnp.concatenate([back[:, :, :256], back[:, :, 256:]], axis=1)
    t_copies = []
    for k, (dz, dc) in enumerate(zc):
        to = peer(dz=dz, dc=dc)
        t_copies.append(net.put(t.at[2 * to[2] + to[3]], t_in.at[k], to))

    landed(weight_z)
    block = weight_out.at[wrows, mine]
    weight_x = [net.put(block, block, peer(dx=o)) for o in range(1, NX)]
    final = [net.put(block, block, peer(dc=1))]

    landed(t_copies)
    total = t[pl.ds(2 * z + c, 1)][0]
    for k in range(len(zc)):
        total = total + t_in[k]
    item[pl.ds(y, 1)] = total[None]
    item_copies = [net.put(item.at[y], item.at[y], peer(dy=o)) for o in range(1, NY)]

    for o in range(1, NX):
        weight_x[o - 1].wait_recv()
        block = weight_out.at[pl.ds(at16(128 * ring(x, -o, NX)), 128), mine]
        final.append(net.put(block, block, peer(dc=1)))
    landed(item_copies)
    for k in range(NY):
        item_out[:, 512 * k:512 * k + 256] = item[k, :4]
        item_out[:, 512 * k + 256:512 * k + 512] = item[k, 4:]
    landed(final)
    net.drain()


def grads(s, q, r, ce, posx, ugain, uweight):
    return pl.pallas_call(
        grads_kernel,
        out_shape=(
            jax.ShapeDtypeStruct((4, HV), F32),
            jax.ShapeDtypeStruct((512, HV), BF16),
        ),
        in_specs=[VM, VM, VM, ANY, VM, VM, ANY],
        out_specs=(VM, VM),
        scratch_shapes=[
            pltpu.VMEM((256, 128), BF16),
            pltpu.VMEM((512, 128), BF16),
            pltpu.VMEM((256, 1024), BF16),
            pltpu.VMEM((256, 1024), BF16),
            pltpu.VMEM((4, 32, HV), BF16),
            pltpu.VMEM((256, 1024), BF16),
            pltpu.VMEM((256, 1024), BF16),
            pltpu.VMEM((4, 32, HV), BF16),
            pltpu.VMEM((3, 64, 1024), BF16),
            pltpu.VMEM((3, 4, 32, 512), BF16),
            pltpu.VMEM((3, 64, 1024), BF16),
            pltpu.VMEM((64, 1024), BF16),
            pltpu.VMEM((4, 32, 512), BF16),
            pltpu.VMEM((64, 1024), BF16),
            pltpu.VMEM((3, 16, 1024), BF16),
            pltpu.VMEM((3, 32, 512), BF16),
            pltpu.VMEM((7, 64, 128), BF16),
            pltpu.VMEM((16, 1024), BF16),
            pltpu.VMEM((32, 512), F32),
            pltpu.VMEM((7, 16, 128), BF16),
            pltpu.VMEM((16, 64, 128), BF16),
            pltpu.VMEM((16, 16, 128), BF16),
            pltpu.VMEM((16, 8, 256), F32),
            pltpu.VMEM((15, 8, 256), F32),
            pltpu.VMEM((4, 8, 256), F32),
            pltpu.SemaphoreType.DMA((C_COPIES,)),
            pltpu.SemaphoreType.DMA((C_COPIES,)),
            pltpu.SemaphoreType.DMA((2,)),
        ],
        compiler_params=pltpu.CompilerParams(
            collective_id=1, has_side_effects=True, vmem_limit_bytes=40 * 2**20
        ),
        name="grads",
    )(s, q, r.reshape(4, 2, 32, HV), ce, posx, ugain, uweight)


def local(
    item_states, item_scores, item_lengths, item_gain, value_weight,
    user_items, negatives, position_embed, user_gain, user_weight,
):
    ugain = user_gain.reshape(1, HV)
    ids = jnp.broadcast_to(user_items, (8, 256))
    ce, pp, posx, nxt = items(
        item_lengths, item_states, item_scores, item_gain.reshape(1, -1), value_weight,
        position_embed, ugain, user_weight, ids,
    )
    targets = jnp.concatenate([user_items[:, 1:], nxt[:1, :1]], axis=1)
    spots = lax.axis_index("fsdp") * 256 + jnp.arange(256)[None, :]
    valid = (spots < ULEN - 1).astype(F32)
    s, q, r = users(user_items, targets, negatives, valid, ce, pp, position_embed)
    return grads(s, q, r, ce, posx, ugain, user_weight)


def solution(mesh):
    return jax.shard_map(
        local,
        mesh=mesh,
        in_specs=(
            P("dp", None, "fsdp"), P("dp", None, None), P("dp"), P("fsdp"), P("fsdp", None),
            P("dp", "fsdp"), P("dp", None), P("fsdp", None), P(), P("fsdp", None),
        ),
        out_specs=(P("dp", None), P("fsdp", None)),
        check_vma=False,
    )
```

```python
import jax
import jax.numpy as jnp
from jax import lax
from jax.experimental import pallas as pl
from jax.experimental.pallas import tpu as pltpu
from jax.sharding import PartitionSpec as P

MESH = pl.DeviceIdType.MESH
F32, BF16 = jnp.float32, jnp.bfloat16
NX, NY, NZ = 4, 4, 8
D, HV, ULEN, USERS = 4096, 2048, 1024, 64
TILES, CHUNK = 4, 512
VM = pl.BlockSpec(memory_space=pltpu.VMEM)
ANY = pl.BlockSpec(memory_space=pl.ANY)
COPIES = 208


def place():
    d, y = lax.axis_index("dp"), lax.axis_index("fsdp")
    return lax.div(d, 16), y, lax.rem(lax.div(d, 2), 8), lax.rem(d, 2)


def ring(i, o, n):
    return lax.rem(i + o + n, n)


def at128(i):
    return pl.multiple_of(i, 128)


def at16(i):
    return pl.multiple_of(i, 16)


def nt(a, b):
    return lax.dot_general(a, b, (((1,), (1,)), ((), ())), preferred_element_type=F32)


def tn(a, b):
    return lax.dot_general(a, b, (((0,), (0,)), ((), ())), preferred_element_type=F32)


def mm(a, b):
    return jnp.dot(a, b, preferred_element_type=F32)


def split(v):
    hi = v.astype(BF16)
    return hi, (v - hi.astype(F32)).astype(BF16)


def meet(peers):
    barrier = pltpu.get_barrier_semaphore()
    for x, y, z, c in peers:
        pl.semaphore_signal(barrier, inc=1, device_id=((x * NZ + z) * 2 + c, y), device_id_type=MESH)
    pl.semaphore_wait(barrier, len(peers))


class Net:
    def __init__(self, send, recv):
        self.send, self.recv, self.all = send, recv, []

    def put(self, src, dst, where):
        x, y, z, c = where
        k = len(self.all)
        assert k < COPIES
        copy = pltpu.make_async_remote_copy(
            src_ref=src,
            dst_ref=dst,
            send_sem=self.send.at[k],
            recv_sem=self.recv.at[k],
            device_id=((x * NZ + z) * 2 + c, y),
            device_id_type=MESH,
        )
        copy.start()
        self.all.append(copy)
        return copy

    def drain(self):
        for copy in self.all:
            copy.wait_send()


def landed(copies):
    for copy in copies:
        copy.wait_recv()


def added(own, parts, count):
    total = own.astype(F32)
    for k in range(count):
        total = total + parts[k].astype(F32)
    return total


def whole_kernel(
    lengths, states_h, scores_h, igain, vweight_h, pos_h, ugain, uweight_h, ids, negs,
    item_out, weight_out,
    states, scores, vweight, uweight, pos, ids8,
    squares, squares_in, num, num_in, cat, ep, ep_in, pin, pback, pback_in, posx, nxt, ce, pp,
    in_v, ep_v, u_v, uh_v, ug_v, iu_v,
    s, q, r, s1_in, q1_in, r1_in, s1, q1, r1, s2_in, r2_in, q2_in, s2, r2, q2, s3_in, r3_in, q3_in, s3, s4_in,
    qg, sg, t, t_in, item,
    send, recv, local,
):
    x, y, z, c = place()
    low = lax.rem(z, 2)
    group = 4 * x + lax.div(z, 2)
    member, quarter = 2 * low + c, 2 * c + low
    base = z - low
    net = Net(send, recv)

    def peer(dx=0, dy=0, dz=0, dc=0):
        return ring(x, dx, NX), ring(y, dy, NY), ring(z, dz, NZ), ring(c, dc, 2)

    def mate(om, oy):
        m = ring(member, om, 4)
        return x, ring(y, oy, NY), base + lax.div(m, 2), lax.rem(m, 2)

    rows16, rows64 = pl.ds(at16(16 * group), 16), pl.ds(at16(64 * x), 64)
    mine, theirs = pl.ds(at128(256 * c), 256), pl.ds(at128(256 * ring(c, 1, 2)), 256)
    own512 = pl.ds(at128(512 * y), 512)
    loads = [
        pltpu.make_async_copy(states_h, states, local.at[0]),
        pltpu.make_async_copy(pos_h.at[rows16, own512], pin.at[0], local.at[1]),
        pltpu.make_async_copy(uweight_h, uweight, local.at[2]),
        pltpu.make_async_copy(scores_h, scores, local.at[3]),
        pltpu.make_async_copy(vweight_h, vweight, local.at[4]),
        pltpu.make_async_copy(pos_h.at[:, pl.ds(at128(512 * y + 128 * x), 128)], posx.at[y], local.at[5]),
        pltpu.make_async_copy(pos_h, pos, local.at[6]),
    ]
    for load in loads:
        load.start()
    ids8[...] = jnp.broadcast_to(ids[...], (8, 256))
    offsets = [(om, oy) for om in range(4) for oy in range(4) if om or oy]
    zs, xs, ys = range(1, NZ), range(1, NX), range(1, NY)
    zc = [(dz, dc) for dc in range(2) for dz in range(NZ) if dz or dc]
    xy = [(dx, dy) for dx in range(NX) for dy in range(NY) if dx or dy]
    meet(
        [mate(om, oy) for om, oy in offsets]
        + [peer(dz=dz, dc=dc) for dz, dc in zc]
        + [peer(dx=dx, dy=dy) for dx, dy in xy]
    )

    pin_copies = [
        net.put(pos_h.at[rows16, pl.ds(at128(512 * ring(y, o, NY)), 512)], pin.at[o], peer(dy=o)) for o in ys
    ]

    loads[0].wait()
    ones = jnp.ones((8, 128), BF16)
    item_row = lax.broadcasted_iota(jnp.int32, (8, 256), 0)
    sums = jnp.zeros((8, 256), F32)
    for i in range(4):
        part = jnp.zeros((256, 128), F32)
        for j in range(8):
            v = states[i, :, 128 * j:128 * (j + 1)].astype(F32)
            part = part + v * v
        hi, lo = split(part)
        rest = (part - hi.astype(F32) - lo.astype(F32)).astype(BF16)
        sums = jnp.where(item_row == i, nt(ones, hi) + nt(ones, lo) + nt(ones, rest), sums)
    squares[...] = sums
    square_copies = [net.put(squares, squares_in.at[o - 1], peer(dy=o)) for o in ys]

    loads[1].wait()
    loads[2].wait()
    landed(pin_copies)
    gain_part = ugain[:, own512]
    pos_rows = pin[...].astype(F32).reshape(64, 512) * gain_part
    pback[...] = mm(
        pos_rows.astype(BF16), uweight[:, pl.ds(at128(512 * quarter), 512)]
    ).reshape(4, 16, 512)
    back_copies = [net.put(pback.at[o], pback_in.at[o - 1], peer(dy=-o)) for o in ys]

    loads[3].wait()
    landed(square_copies)
    inv_rms = lax.rsqrt((squares[...] + squares_in[0] + squares_in[1] + squares_in[2]) / D + 1e-05)
    token = lax.broadcasted_iota(jnp.int32, (16, 256), 1)
    pooled_hi, pooled_lo = [], []
    for i in range(4):
        weights = jnp.where(token < lengths[i], jnp.exp(scores[i]), 0.0)
        weights = weights * (inv_rms[i:i + 1] / jnp.sum(weights, axis=1, keepdims=True))
        hi, lo = split(weights)
        both = mm(jnp.concatenate([hi, lo], axis=0), states[i])
        pooled = (both[:16] + both[16:]) * igain[...]
        hi, lo = split(pooled)
        pooled_hi.append(hi)
        pooled_lo.append(lo)
    left = jnp.concatenate(pooled_hi + pooled_lo, axis=0)
    loads[4].wait()
    head = lax.broadcasted_iota(jnp.int32, (4, 16, 256), 1)
    tile = lax.broadcasted_iota(jnp.int32, (4, 16, 256), 2) // 128
    for j in range(8):
        full = mm(left, vweight[:, 256 * j:256 * (j + 1)])
        full = (full[:64] + full[64:]).reshape(4, 16, 256)
        block = jnp.sum(jnp.where(head == tile + 2 * j, full, 0.0), axis=1)
        num[j // 2, 4 * (j % 2):4 * (j % 2) + 4, :] = block
    num_copies = []
    for om, oy in offsets:
        num_copies.append(net.put(num.at[ring(y, oy, NY)], num_in.at[oy, member], mate(om, oy)))
    num_in[0, pl.ds(member, 1)] = num[pl.ds(y, 1)]

    landed(back_copies)
    pp[pl.ds(quarter, 1), rows16] = (pback[0] + pback_in[0] + pback_in[1] + pback_in[2]).astype(BF16)[None]
    own = pp.at[quarter, rows16]
    pp_z = [net.put(own, own, peer(dz=o)) for o in zs]

    landed(num_copies)
    for m in range(4):
        total = num_in[0, m] + num_in[1, m] + num_in[2, m] + num_in[3, m]
        cat[4 * m:4 * m + 4, :256] = total[:4]
        cat[4 * m:4 * m + 4, 256:] = total[4:]
    embed = cat[...].astype(BF16)
    gained = (embed.astype(F32) * gain_part).astype(BF16)
    for k in range(NY):
        ep[k] = mm(gained, uweight[:, pl.ds(at128(512 * k + 128 * quarter), 128)])
    ep_copies = [net.put(ep.at[ring(y, o, NY)], ep_in.at[o - 1], peer(dy=o)) for o in ys]
    part = pl.ds(at128(128 * quarter), 128)
    ce[0, pl.ds(y, 1), rows16, part] = cat[:, part].astype(BF16)[None]
    block = ce.at[0, y, rows16, part]
    cat_z = [net.put(block, block, peer(dz=o)) for o in zs]

    landed(pp_z)
    own = pp.at[pl.ds(2 * c, 2), rows64]
    pp_x = [net.put(own, own, peer(dx=o)) for o in xs]

    landed(ep_copies)
    ce[1, pl.ds(y, 1), rows16, part] = (ep[pl.ds(y, 1)] + ep_in[0] + ep_in[1] + ep_in[2]).astype(BF16)
    block = ce.at[1, y, rows16, part]
    ep_z = [net.put(block, block, peer(dz=o)) for o in zs]

    landed(cat_z)
    block = ce.at[0, y, rows64, mine]
    cat_x = [net.put(block, block, peer(dx=o)) for o in xs]
    landed(ep_z)
    block = ce.at[1, y, rows64, mine]
    ep_y = [net.put(block, block, peer(dy=o)) for o in ys]

    landed(pp_x)
    own = pp.at[pl.ds(2 * c, 2)]
    final = [net.put(own, own, peer(dc=1))]

    landed(cat_x)
    block = ce.at[0, y, :, mine]
    cat_y = [net.put(block, block, peer(dy=o)) for o in ys]
    final.append(net.put(block, block, peer(dc=1)))
    landed(ep_y)
    block = ce.at[1, :, rows64, mine]
    ep_x = [net.put(block, block, peer(dx=o)) for o in xs]
    final.append(net.put(block, block, peer(dc=1)))
    for o in ys:
        cat_y[o - 1].wait_recv()
        block = ce.at[0, ring(y, -o, NY), :, mine]
        final.append(net.put(block, block, peer(dc=1)))
    for o in xs:
        ep_x[o - 1].wait_recv()
        block = ce.at[1, :, pl.ds(at16(64 * ring(x, -o, NX)), 64), mine]
        final.append(net.put(block, block, peer(dc=1)))
    next_copy = net.put(ids8, nxt, peer(dy=-1))
    posx_copies = [
        net.put(pos_h.at[:, pl.ds(at128(512 * ring(y, o, NY) + 128 * x), 128)], posx.at[y], peer(dy=o)) for o in ys
    ]
    landed(final)
    landed([next_copy])
    loads[6].wait()

    js = [slice(CHUNK * k, CHUNK * (k + 1)) for k in range(TILES)]
    all_items = lax.broadcasted_iota(jnp.int32, (256, 256), 0)
    hot_t32 = (all_items == ids[...]).astype(F32)
    hot_t = hot_t32.astype(BF16)
    hot = hot_t32.T.astype(BF16)
    lane = lax.broadcasted_iota(jnp.int32, (8, 256), 1)
    targets = jnp.where(lane == 255, pltpu.roll(nxt[...], 255, 1), pltpu.roll(ids8[...], 255, 1))[:1]
    target_t = (all_items == targets).astype(F32)
    counts = jnp.sum((all_items == negs[...]).astype(F32), axis=1, keepdims=True)
    spots = y * 256 + lax.broadcasted_iota(jnp.int32, (1, 256), 1)
    scale = jnp.where(spots < ULEN - 1, 1.0 / (USERS * (ULEN - 1)), 0.0)

    in_squares = jnp.zeros((256, 1), F32)
    cat_squares = jnp.zeros((256, 1), F32)
    for k, j in enumerate(js):
        v = mm(hot, ce[0, k]) + pos[:, j].astype(F32)
        in_v[:, j] = v
        in_squares += jnp.sum(v * v, axis=1, keepdims=True)
        w = ce[0, k].astype(F32)
        cat_squares += jnp.sum(w * w, axis=1, keepdims=True)
    inv = lax.rsqrt(in_squares / HV + 1e-05)
    cat_inv = 1.0 / jnp.sqrt(cat_squares + 1e-06)
    out_squares = jnp.zeros((256, 1), F32)
    for k, j in enumerate(js):
        e = mm(hot, ce[1, k]) + pp[k].astype(F32)
        ep_v[:, j] = e
        v = in_v[:, j] + inv * e
        u_v[:, j] = v
        out_squares += jnp.sum(v * v, axis=1, keepdims=True)
    out_inv = 1.0 / jnp.sqrt(out_squares + 1e-06)
    logits = jnp.zeros((256, 256), F32)
    for k, j in enumerate(js):
        u = u_v[:, j] * out_inv
        u_v[:, j] = u
        hi, lo = split(u)
        uh_v[:, j] = hi
        logits += nt(ce[0, k], hi) + nt(ce[0, k], lo)
    powers = jnp.exp(20.0 * cat_inv * logits)
    pos_power = jnp.sum(target_t * powers, axis=0, keepdims=True)
    total = pos_power + jnp.sum(counts * powers, axis=0, keepdims=True)
    grad_t = scale * (counts * powers / total + target_t * (pos_power / total - 1.0))
    by_item = grad_t.astype(BF16)
    by_row_hi, by_row_lo = split((grad_t * cat_inv).T)
    along = jnp.zeros((256, 1), F32)
    cat_along = jnp.zeros((256, 1), F32)
    for k, j in enumerate(js):
        v = 20.0 * (mm(by_row_hi, ce[0, k]) + mm(by_row_lo, ce[0, k]))
        ug_v[:, j] = v
        along += jnp.sum(v * u_v[:, j], axis=1, keepdims=True)
        v = 20.0 * mm(by_item, uh_v[:, j])
        iu_v[:, j] = v
        cat_along += jnp.sum(v * ce[0, k].astype(F32), axis=1, keepdims=True)
    cat_along = cat_along * cat_inv * cat_inv
    inner = jnp.zeros((256, 1), F32)
    for j in js:
        g = (ug_v[:, j] - u_v[:, j] * along) * out_inv
        ug_v[:, j] = g
        inner += jnp.sum(g * ep_v[:, j], axis=1, keepdims=True)
    inner = inner * (inv * inv * inv / HV)
    s1_copies, q1_copies, r1_copies = [], [], []
    for k, j in enumerate(js):
        g = ug_v[:, j]
        rows = (inv * g).astype(BF16)
        q[k] = rows
        q1_copies.append(net.put(q.at[k, :, theirs], q1_in.at[k], peer(dc=1)))
        s[k] = mm(hot_t, rows).astype(BF16)
        s1_copies.append(net.put(s.at[k, :, theirs], s1_in.at[k], peer(dc=1)))
        direct = (g - in_v[:, j] * inner).astype(BF16)
        item_grad = (iu_v[:, j] - ce[0, k].astype(F32) * cat_along) * cat_inv
        r[k] = (mm(hot_t, direct) + item_grad).astype(BF16)
        r1_copies.append(net.put(r.at[k, :, theirs], r1_in.at[k], peer(dc=1)))

    for k in range(TILES):
        q1_copies[k].wait_recv()
        q1[k] = (q[k, :, mine].astype(F32) + q1_in[k].astype(F32)).astype(BF16)
        s1_copies[k].wait_recv()
        s1[k] = (s[k, :, mine].astype(F32) + s1_in[k].astype(F32)).astype(BF16)
        r1_copies[k].wait_recv()
        r1[k] = (r[k, :, mine].astype(F32) + r1_in[k].astype(F32)).astype(BF16)
    s2_copies = [net.put(s1.at[:, pl.ds(at16(64 * ring(y, o, NY)), 64)], s2_in.at[o - 1], peer(dy=o)) for o in ys]
    q2_copies = [net.put(q1.at[:, pl.ds(at16(64 * ring(x, o, NX)), 64)], q2_in.at[o - 1], peer(dx=o)) for o in xs]
    r2_copies = [net.put(r1.at[ring(y, o, NY)], r2_in.at[o - 1], peer(dy=o)) for o in ys]

    landed(s2_copies)
    s2[...] = added(s1[:, pl.ds(at16(64 * y), 64)], s2_in, 3).astype(BF16)
    s3_copies = [net.put(s2.at[:, pl.ds(at16(16 * ring(x, o, NX)), 16)], s3_in.at[o - 1], peer(dx=o)) for o in xs]
    landed(q2_copies)
    q2[...] = added(q1[:, rows64], q2_in, 3).astype(BF16)

    def slot(to):
        return lax.div(to, 2), pl.ds(at128(128 * lax.rem(to, 2)), 128)

    q3_copies = []
    for o in zs:
        k, part = slot(ring(z, o, NZ))
        q3_copies.append(net.put(q2.at[k, :, part], q3_in.at[o - 1], peer(dz=o)))
    landed(r2_copies)
    r2[...] = added(r1[pl.ds(y, 1)][0], r2_in, 3).astype(BF16)
    r3_copies = [net.put(r2.at[pl.ds(at16(64 * ring(x, o, NX)), 64)], r3_in.at[o - 1], peer(dx=o)) for o in xs]
    landed(s3_copies)
    s3[...] = added(s2[:, pl.ds(at16(16 * x), 16)], s3_in, 3).astype(BF16)
    s4_copies = []
    for o in zs:
        k, part = slot(ring(z, o, NZ))
        s4_copies.append(net.put(s3.at[k, :, part], s4_in.at[o - 1], peer(dz=o)))
    spot = 4 * y + x
    own, part = slot(z)
    landed(q3_copies)
    qg[pl.ds(spot, 1)] = added(q2[pl.ds(own, 1), :, part][0], q3_in, NZ - 1).astype(BF16)[None]
    qg_copies = [net.put(qg.at[spot], qg.at[spot], peer(dx=dx, dy=dy)) for dx, dy in xy]
    landed(s4_copies)
    sg[pl.ds(spot, 1)] = added(s3[pl.ds(own, 1), :, part][0], s4_in, NZ - 1).astype(BF16)[None]
    sg_copies = [net.put(sg.at[spot], sg.at[spot], peer(dx=dx, dy=dy)) for dx, dy in xy]
    landed(r3_copies)
    r3 = added(r2[rows64], r3_in, 3)

    gain_rows = ugain[:, pl.ds(at128(512 * y + 128 * x), 128)]
    loads[5].wait()
    landed(posx_copies)
    positions = (posx[...].astype(F32).reshape(1024, 128) * gain_rows).astype(BF16)
    embeds = (ce[0, pl.ds(y, 1), :, pl.ds(at128(128 * x), 128)][0].astype(F32) * gain_rows).astype(BF16)
    landed(qg_copies)
    tile = tn(positions, qg[...].reshape(1024, 128))
    landed(sg_copies)
    tile = tile + tn(embeds, sg[...].reshape(256, 128))
    wrows = pl.ds(at16(128 * x), 128)
    zcols = pl.ds(at128(512 * lax.div(z, 2) + 256 * c + 128 * low), 128)
    weight_out[wrows, zcols] = tile.astype(BF16)
    block = weight_out.at[wrows, zcols]
    weight_z = [net.put(block, block, peer(dz=o)) for o in zs]

    back = nt(sg[pl.ds(4 * x, 4)].reshape(64, 128), uweight[:, zcols]) * gain_part
    half = lax.broadcasted_iota(jnp.int32, (64, 512), 1) // 256
    back = back + jnp.where(half == c, jnp.concatenate([r3, r3], axis=1), 0.0)
    back = back.reshape(16, 4, 512)
    t[...] = jnp.concatenate([back[:, :, :256], back[:, :, 256:]], axis=1)
    t_copies = []
    for k, (dz, dc) in enumerate(zc):
        to = peer(dz=dz, dc=dc)
        t_copies.append(net.put(t.at[2 * to[2] + to[3]], t_in.at[k], to))

    landed(weight_z)
    weight_x, final = [], []
    for k in range(TILES):
        block = weight_out.at[wrows, pl.ds(at128(512 * k + 256 * c), 256)]
        weight_x.append([net.put(block, block, peer(dx=o)) for o in xs])
        final.append(net.put(block, block, peer(dc=1)))

    landed(t_copies)
    total = added(t[pl.ds(2 * z + c, 1)][0], t_in, len(zc))
    item[pl.ds(y, 1)] = total[None]
    item_copies = [net.put(item.at[y], item.at[y], peer(dy=o)) for o in ys]

    for k in range(TILES):
        for o in xs:
            weight_x[k][o - 1].wait_recv()
            rows = pl.ds(at16(128 * ring(x, -o, NX)), 128)
            block = weight_out.at[rows, pl.ds(at128(512 * k + 256 * c), 256)]
            final.append(net.put(block, block, peer(dc=1)))
    landed(item_copies)
    for k in range(NY):
        item_out[:, 512 * k:512 * k + 256] = item[k, :4]
        item_out[:, 512 * k + 256:512 * k + 512] = item[k, 4:]
    landed(final)
    net.drain()


def local(
    item_states, item_scores, item_lengths, item_gain, value_weight,
    user_items, negatives, position_embed, user_gain, user_weight,
):
    def vm(*shape, dtype=BF16):
        return pltpu.VMEM(shape, dtype)

    return pl.pallas_call(
        whole_kernel,
        out_shape=(vm(4, HV, dtype=F32), vm(512, HV)),
        in_specs=[pl.BlockSpec(memory_space=pltpu.SMEM), ANY, ANY, VM, ANY, ANY, VM, ANY, VM, VM],
        out_specs=(VM, VM),
        scratch_shapes=[
            vm(4, 256, 1024), vm(4, 16, 256, dtype=F32), vm(1024, HV), vm(512, HV), vm(256, HV),
            vm(8, 256, dtype=jnp.int32),
            vm(8, 256, dtype=F32), vm(3, 8, 256, dtype=F32),
            vm(4, 8, 256, dtype=F32), vm(4, 4, 8, 256, dtype=F32), vm(16, 512, dtype=F32),
            vm(4, 16, 128, dtype=F32), vm(3, 16, 128, dtype=F32),
            vm(4, 16, 512), vm(4, 16, 512, dtype=F32), vm(3, 16, 512, dtype=F32),
            vm(4, 256, 128), vm(8, 256, dtype=jnp.int32),
            vm(2, 4, 256, 512), vm(4, 256, 512),
            vm(256, HV, dtype=F32), vm(256, HV, dtype=F32), vm(256, HV, dtype=F32), vm(256, HV),
            vm(256, HV, dtype=F32), vm(256, HV, dtype=F32),
            vm(4, 256, 512), vm(4, 256, 512), vm(4, 256, 512),
            vm(4, 256, 256), vm(4, 256, 256), vm(4, 256, 256),
            vm(4, 256, 256), vm(4, 256, 256), vm(4, 256, 256),
            vm(3, 4, 64, 256), vm(3, 256, 256), vm(3, 4, 64, 256),
            vm(4, 64, 256), vm(256, 256), vm(4, 64, 256),
            vm(3, 4, 16, 256), vm(3, 64, 256), vm(7, 64, 128),
            vm(4, 16, 256), vm(7, 16, 128),
            vm(16, 64, 128), vm(16, 16, 128),
            vm(16, 8, 256, dtype=F32), vm(15, 8, 256, dtype=F32), vm(4, 8, 256, dtype=F32),
            pltpu.SemaphoreType.DMA((COPIES,)),
            pltpu.SemaphoreType.DMA((COPIES,)),
            pltpu.SemaphoreType.DMA((7,)),
        ],
        compiler_params=pltpu.CompilerParams(
            collective_id=0, has_side_effects=True, vmem_limit_bytes=60 * 2**20
        ),
        name="whole",
    )(
        item_lengths, item_states, item_scores, item_gain.reshape(1, -1), value_weight,
        position_embed, user_gain.reshape(1, HV), user_weight, user_items, negatives,
    )


def solution(mesh):
    return jax.shard_map(
        local,
        mesh=mesh,
        in_specs=(
            P("dp", None, "fsdp"), P("dp", None, None), P("dp"), P("fsdp"), P("fsdp", None),
            P("dp", "fsdp"), P("dp", None), P("fsdp", None), P(), P("fsdp", None),
        ),
        out_specs=(P("dp", None), P("fsdp", None)),
        check_vma=False,
    )
```

```python
import jax
import jax.numpy as jnp
from jax import lax
from jax.experimental import pallas as pl
from jax.experimental.pallas import tpu as pltpu
from jax.sharding import PartitionSpec as P

MESH = pl.DeviceIdType.MESH
F32, BF16 = jnp.float32, jnp.bfloat16
NX, NY, NZ = 4, 4, 8
D, HV, ULEN, USERS = 4096, 2048, 1024, 64
TILES, CHUNK = 4, 512
VM = pl.BlockSpec(memory_space=pltpu.VMEM)
ANY = pl.BlockSpec(memory_space=pl.ANY)
COPIES = 250


def place():
    d, y = lax.axis_index("dp"), lax.axis_index("fsdp")
    return lax.div(d, 16), y, lax.rem(lax.div(d, 2), 8), lax.rem(d, 2)


def ring(i, o, n):
    return lax.rem(i + o + n, n)


def at128(i):
    return pl.multiple_of(i, 128)


def at16(i):
    return pl.multiple_of(i, 16)


def nt(a, b):
    return lax.dot_general(a, b, (((1,), (1,)), ((), ())), preferred_element_type=F32)


def tn(a, b):
    return lax.dot_general(a, b, (((0,), (0,)), ((), ())), preferred_element_type=F32)


def mm(a, b):
    return jnp.dot(a, b, preferred_element_type=F32)


def split(v):
    hi = v.astype(BF16)
    return hi, (v - hi.astype(F32)).astype(BF16)


def greet(peers):
    barrier = pltpu.get_barrier_semaphore()
    for x, y, z, c in peers:
        pl.semaphore_signal(barrier, inc=1, device_id=((x * NZ + z) * 2 + c, y), device_id_type=MESH)
    return barrier, len(peers)


class Net:
    def __init__(self, send, recv):
        self.send, self.recv, self.all, self.sent = send, recv, [], 0

    def put(self, src, dst, where):
        x, y, z, c = where
        k = len(self.all)
        assert k < COPIES
        copy = pltpu.make_async_remote_copy(
            src_ref=src,
            dst_ref=dst,
            send_sem=self.send.at[k],
            recv_sem=self.recv.at[k],
            device_id=((x * NZ + z) * 2 + c, y),
            device_id_type=MESH,
        )
        copy.start()
        self.all.append(copy)
        return copy

    def drain(self, upto=None):
        upto = len(self.all) if upto is None else upto
        for copy in self.all[self.sent:upto]:
            copy.wait_send()
        self.sent = upto


def landed(copies):
    for copy in copies:
        copy.wait_recv()


def added(own, parts, count):
    total = own.astype(F32)
    for k in range(count):
        total = total + parts[k].astype(F32)
    return total


def whole_kernel(
    lengths_h, states_h, scores_h, igain_h, vweight_h, pos_h, ugain_h, uweight_h, ids_h, negs_h,
    item_out, weight_out,
    lengths, igain, ugain, ids, negs, states, scores, vweight, uweight, pos, ids8,
    squares, squares_in, num, num_in, cat, ep, ep_in, pin, pback, pback_in, posx, nxt, ce, pp,
    in_v, ep_v, u_v, uh_v, ug_v, iu_v,
    s, q, r, s1_in, q1_in, r1_in, s1, q1, r1, s2_in, r2_in, q2_in, s2, r2, q2, s3_in, r3_in, q3_in, s3, s4_in,
    qg, sg, t, t_in, t2, t2_in, item,
    send, recv, local,
):
    x, y, z, c = place()
    low = lax.rem(z, 2)
    group = 4 * x + lax.div(z, 2)
    member, quarter = 2 * low + c, 2 * c + low
    base = z - low
    net = Net(send, recv)

    def peer(dx=0, dy=0, dz=0, dc=0):
        return ring(x, dx, NX), ring(y, dy, NY), ring(z, dz, NZ), ring(c, dc, 2)

    def mate(om, oy):
        m = ring(member, om, 4)
        return x, ring(y, oy, NY), base + lax.div(m, 2), lax.rem(m, 2)

    rows16, rows64 = pl.ds(at16(16 * group), 16), pl.ds(at16(64 * x), 64)
    mine, theirs = pl.ds(at128(256 * c), 256), pl.ds(at128(256 * ring(c, 1, 2)), 256)
    own512 = pl.ds(at128(512 * y), 512)
    loads = [
        pltpu.make_async_copy(states_h, states, local.at[0]),
        pltpu.make_async_copy(pos_h.at[rows16, own512], pin.at[0], local.at[1]),
        pltpu.make_async_copy(uweight_h, uweight, local.at[2]),
        pltpu.make_async_copy(scores_h, scores, local.at[3]),
        pltpu.make_async_copy(vweight_h, vweight, local.at[4]),
        pltpu.make_async_copy(pos_h.at[:, pl.ds(at128(512 * y + 128 * x), 128)], posx.at[y], local.at[5]),
        pltpu.make_async_copy(pos_h, pos, local.at[6]),
        pltpu.make_async_copy(lengths_h, lengths, local.at[7]),
        pltpu.make_async_copy(igain_h, igain, local.at[8]),
        pltpu.make_async_copy(ugain_h, ugain, local.at[9]),
        pltpu.make_async_copy(ids_h, ids, local.at[10]),
        pltpu.make_async_copy(negs_h, negs, local.at[11]),
    ]
    loads[0].start()
    offsets = [(om, oy) for om in range(4) for oy in range(4) if om or oy]
    zs, xs, ys = range(1, NZ), range(1, NX), range(1, NY)
    xy = [(dx, dy) for dx in range(NX) for dy in range(NY) if dx or dy]
    barrier, count = greet(
        [mate(om, oy) for om, oy in offsets]
        + [peer(dz=o) for o in zs]
        + [peer(dx=dx, dy=dy) for dx, dy in xy if dx]
    )
    for load in loads[7:]:
        load.start()
    for load in loads[1:7]:
        load.start()
    for load in loads[7:]:
        load.wait()
    ids8[...] = jnp.broadcast_to(ids[...], (8, 256))

    loads[0].wait()
    ones = jnp.ones((8, 128), BF16)
    item_row = lax.broadcasted_iota(jnp.int32, (8, 256), 0)
    sums = jnp.zeros((8, 256), F32)
    for i in range(4):
        part = jnp.zeros((256, 128), F32)
        for j in range(8):
            v = states[i, :, 128 * j:128 * (j + 1)].astype(F32)
            part = part + v * v
        hi, lo = split(part)
        rest = (part - hi.astype(F32) - lo.astype(F32)).astype(BF16)
        sums = jnp.where(item_row == i, nt(ones, hi) + nt(ones, lo) + nt(ones, rest), sums)
    squares[...] = sums
    pl.semaphore_wait(barrier, count)
    square_copies = [net.put(squares, squares_in.at[o - 1], peer(dy=o)) for o in ys]
    pin_copies = [
        net.put(pos_h.at[rows16, pl.ds(at128(512 * ring(y, o, NY)), 512)], pin.at[o], peer(dy=o)) for o in ys
    ]
    next_copy = net.put(ids8, nxt, peer(dy=-1))
    loads[3].wait()
    token = lax.broadcasted_iota(jnp.int32, (16, 256), 1)
    for i in range(4):
        weights = jnp.where(token < lengths[i], jnp.exp(scores[i]), 0.0)
        scores[i] = weights / jnp.sum(weights, axis=1, keepdims=True)

    loads[1].wait()
    loads[2].wait()
    landed(pin_copies)
    gain_part = ugain[:, own512]
    pos_rows = pin[...].astype(F32).reshape(64, 512) * gain_part
    pback[...] = mm(
        pos_rows.astype(BF16), uweight[:, pl.ds(at128(512 * quarter), 512)]
    ).reshape(4, 16, 512)
    back_copies = [net.put(pback.at[o], pback_in.at[o - 1], peer(dy=-o)) for o in ys]

    landed(square_copies)
    inv_rms = lax.rsqrt((squares[...] + squares_in[0] + squares_in[1] + squares_in[2]) / D + 1e-05)
    pooled_hi, pooled_lo = [], []
    for i in range(4):
        hi, lo = split(scores[i] * inv_rms[i:i + 1])
        both = mm(jnp.concatenate([hi, lo], axis=0), states[i])
        pooled = (both[:16] + both[16:]) * igain[...]
        hi, lo = split(pooled)
        pooled_hi.append(hi)
        pooled_lo.append(lo)
    left = jnp.concatenate(pooled_hi + pooled_lo, axis=0)
    loads[4].wait()
    head = lax.broadcasted_iota(jnp.int32, (4, 16, 256), 1)
    tile = lax.broadcasted_iota(jnp.int32, (4, 16, 256), 2) // 128
    for j in range(8):
        full = mm(left, vweight[:, 256 * j:256 * (j + 1)])
        full = (full[:64] + full[64:]).reshape(4, 16, 256)
        block = jnp.sum(jnp.where(head == tile + 2 * j, full, 0.0), axis=1)
        num[j // 2, 4 * (j % 2):4 * (j % 2) + 4, :] = block
    num_copies = []
    for om, oy in offsets:
        num_copies.append(net.put(num.at[ring(y, oy, NY)], num_in.at[oy, member], mate(om, oy)))
    num_in[0, pl.ds(member, 1)] = num[pl.ds(y, 1)]
    mark = len(net.all) - 15

    landed(back_copies)
    pp[pl.ds(quarter, 1), rows16] = (pback[0] + pback_in[0] + pback_in[1] + pback_in[2]).astype(BF16)[None]
    own = pp.at[quarter, rows16]
    pp_z = [net.put(own, own, peer(dz=o)) for o in zs]

    landed(num_copies)
    for m in range(4):
        total = num_in[0, m] + num_in[1, m] + num_in[2, m] + num_in[3, m]
        cat[4 * m:4 * m + 4, :256] = total[:4]
        cat[4 * m:4 * m + 4, 256:] = total[4:]
    embed = cat[...].astype(BF16)
    gained = (embed.astype(F32) * gain_part).astype(BF16)
    for k in range(NY):
        ep[k] = mm(gained, uweight[:, pl.ds(at128(512 * k + 128 * quarter), 128)])
    ep_copies = [net.put(ep.at[ring(y, o, NY)], ep_in.at[o - 1], peer(dy=o)) for o in ys]
    part = pl.ds(at128(128 * quarter), 128)
    ce[0, pl.ds(y, 1), rows16, part] = cat[:, part].astype(BF16)[None]
    block = ce.at[0, y, rows16, part]
    cat_z = [net.put(block, block, peer(dz=o)) for o in zs]

    landed(pp_z)
    own = pp.at[pl.ds(2 * c, 2), rows64]
    pp_x = [net.put(own, own, peer(dx=o)) for o in xs]

    net.drain(mark)
    mark = len(net.all) - 17
    landed(ep_copies)
    ce[1, pl.ds(y, 1), rows16, part] = (ep[pl.ds(y, 1)] + ep_in[0] + ep_in[1] + ep_in[2]).astype(BF16)
    block = ce.at[1, y, rows16, part]
    ep_z = [net.put(block, block, peer(dz=o)) for o in zs]

    halves = [pl.ds(at128(256 * c + 128 * h), 128) for h in range(2)]

    def second(a):
        by_x = [net.put(ce.at[a, y, rows64, halves[0]], ce.at[a, y, rows64, halves[0]], peer(dx=o)) for o in xs]
        by_y = [net.put(ce.at[a, y, rows64, halves[1]], ce.at[a, y, rows64, halves[1]], peer(dy=o)) for o in ys]
        return by_x, by_y

    def third(a, by_x, by_y):
        landed(by_x)
        block = ce.at[a, y, :, halves[0]]
        to_y = [net.put(block, block, peer(dy=o)) for o in ys]
        landed(by_y)
        block = ce.at[a, :, rows64, halves[1]]
        to_x = [net.put(block, block, peer(dx=o)) for o in xs]
        block = ce.at[a, y, :, halves[0]]
        shared = [net.put(block, block, peer(dc=1))]
        block = ce.at[a, :, rows64, halves[1]]
        shared.append(net.put(block, block, peer(dc=1)))
        return to_y, to_x, shared

    def fourth(a, to_y, to_x, shared):
        for o in range(1, 4):
            to_y[o - 1].wait_recv()
            block = ce.at[a, ring(y, -o, NY), :, halves[0]]
            shared.append(net.put(block, block, peer(dc=1)))
            to_x[o - 1].wait_recv()
            block = ce.at[a, :, pl.ds(at16(64 * ring(x, -o, NX)), 64), halves[1]]
            shared.append(net.put(block, block, peer(dc=1)))
        return shared

    net.drain(mark)
    mark = len(net.all)
    landed(cat_z)
    cat_2 = second(0)
    landed(ep_z)
    ep_2 = second(1)
    landed(pp_x)
    own = pp.at[pl.ds(2 * c, 2)]
    pp_final = net.put(own, own, peer(dc=1))
    cat_3 = third(0, *cat_2)
    ep_3 = third(1, *ep_2)
    cat_4 = fourth(0, *cat_3)
    ep_4 = fourth(1, *ep_3)
    posx_copies = [
        net.put(pos_h.at[:, pl.ds(at128(512 * ring(y, o, NY) + 128 * x), 128)], posx.at[y], peer(dy=o)) for o in ys
    ]
    net.drain(mark)
    mark = len(net.all)
    landed(cat_4)
    landed([next_copy])
    loads[6].wait()

    js = [slice(CHUNK * k, CHUNK * (k + 1)) for k in range(TILES)]
    all_items = lax.broadcasted_iota(jnp.int32, (256, 256), 0)
    hot_t32 = (all_items == ids[...]).astype(F32)
    hot_t = hot_t32.astype(BF16)
    hot = hot_t32.T.astype(BF16)
    lane = lax.broadcasted_iota(jnp.int32, (8, 256), 1)
    targets = jnp.where(lane == 255, pltpu.roll(nxt[...], 255, 1), pltpu.roll(ids8[...], 255, 1))[:1]
    target_t = (all_items == targets).astype(F32)
    counts = jnp.sum((all_items == negs[...]).astype(F32), axis=1, keepdims=True)
    spots = y * 256 + lax.broadcasted_iota(jnp.int32, (1, 256), 1)
    scale = jnp.where(spots < ULEN - 1, 1.0 / (USERS * (ULEN - 1)), 0.0)

    in_squares = jnp.zeros((256, 1), F32)
    cat_squares = jnp.zeros((256, 1), F32)
    for k, j in enumerate(js):
        v = mm(hot, ce[0, k]) + pos[:, j].astype(F32)
        in_v[:, j] = v
        in_squares += jnp.sum(v * v, axis=1, keepdims=True)
        w = ce[0, k].astype(F32)
        cat_squares += jnp.sum(w * w, axis=1, keepdims=True)
    inv = lax.rsqrt(in_squares / HV + 1e-05)
    cat_inv = 1.0 / jnp.sqrt(cat_squares + 1e-06)
    landed(ep_4)
    pp_final.wait_recv()
    out_squares = jnp.zeros((256, 1), F32)
    for k, j in enumerate(js):
        e = mm(hot, ce[1, k]) + pp[k].astype(F32)
        ep_v[:, j] = e
        v = in_v[:, j] + inv * e
        u_v[:, j] = v
        out_squares += jnp.sum(v * v, axis=1, keepdims=True)
    out_inv = 1.0 / jnp.sqrt(out_squares + 1e-06)
    logits = jnp.zeros((256, 256), F32)
    for k, j in enumerate(js):
        u = u_v[:, j] * out_inv
        u_v[:, j] = u
        hi, lo = split(u)
        uh_v[:, j] = hi
        logits += nt(ce[0, k], hi) + nt(ce[0, k], lo)
    powers = jnp.exp(20.0 * cat_inv * logits)
    pos_power = jnp.sum(target_t * powers, axis=0, keepdims=True)
    total = pos_power + jnp.sum(counts * powers, axis=0, keepdims=True)
    grad_t = scale * (counts * powers / total + target_t * (pos_power / total - 1.0))
    by_row_hi, by_row_lo = split((grad_t * cat_inv).T)
    along = jnp.zeros((256, 1), F32)
    for k, j in enumerate(js):
        v = 20.0 * (mm(by_row_hi, ce[0, k]) + mm(by_row_lo, ce[0, k]))
        ug_v[:, j] = v
        along += jnp.sum(v * u_v[:, j], axis=1, keepdims=True)
    inner = jnp.zeros((256, 1), F32)
    s1_copies, q1_copies, r1_copies, s2_copies, q2_copies = [], [], [], [], []

    def chips(k):
        q1_copies[k].wait_recv()
        q1[k] = (q[k, :, mine].astype(F32) + q1_in[k].astype(F32)).astype(BF16)
        for o in xs:
            rows = pl.ds(at16(64 * ring(x, o, NX)), 64)
            q2_copies.append(net.put(q1.at[k, rows], q2_in.at[o - 1, k], peer(dx=o)))
        s1_copies[k].wait_recv()
        s1[k] = (s[k, :, mine].astype(F32) + s1_in[k].astype(F32)).astype(BF16)
        for o in ys:
            rows = pl.ds(at16(64 * ring(y, o, NY)), 64)
            s2_copies.append(net.put(s1.at[k, rows], s2_in.at[o - 1, k], peer(dy=o)))

    for k, j in enumerate(js):
        g = (ug_v[:, j] - u_v[:, j] * along) * out_inv
        ug_v[:, j] = g
        rows = (inv * g).astype(BF16)
        q[k] = rows
        q1_copies.append(net.put(q.at[k, :, theirs], q1_in.at[k], peer(dc=1)))
        s[k] = mm(hot_t, rows).astype(BF16)
        s1_copies.append(net.put(s.at[k, :, theirs], s1_in.at[k], peer(dc=1)))
        inner += jnp.sum(g * ep_v[:, j], axis=1, keepdims=True)
        if k:
            chips(k - 1)
    inner = inner * (inv * inv * inv / HV)
    by_item = grad_t.astype(BF16)
    cat_along = jnp.zeros((256, 1), F32)
    for k, j in enumerate(js):
        v = 20.0 * mm(by_item, uh_v[:, j])
        iu_v[:, j] = v
        cat_along += jnp.sum(v * ce[0, k].astype(F32), axis=1, keepdims=True)
        if k == 0:
            chips(TILES - 1)
    cat_along = cat_along * cat_inv * cat_inv
    for k, j in enumerate(js):
        direct = (ug_v[:, j] - in_v[:, j] * inner).astype(BF16)
        item_grad = (iu_v[:, j] - ce[0, k].astype(F32) * cat_along) * cat_inv
        r[k] = (mm(hot_t, direct) + item_grad).astype(BF16)
        r1_copies.append(net.put(r.at[k, :, theirs], r1_in.at[k], peer(dc=1)))
    for k in range(TILES):
        r1_copies[k].wait_recv()
        r1[k] = (r[k, :, mine].astype(F32) + r1_in[k].astype(F32)).astype(BF16)
    r2_copies = [net.put(r1.at[ring(y, o, NY)], r2_in.at[o - 1], peer(dy=o)) for o in ys]

    net.drain(mark)
    mark = len(net.all)
    landed(s2_copies)
    s2[...] = added(s1[:, pl.ds(at16(64 * y), 64)], s2_in, 3).astype(BF16)
    s3_copies = [net.put(s2.at[:, pl.ds(at16(16 * ring(x, o, NX)), 16)], s3_in.at[o - 1], peer(dx=o)) for o in xs]
    landed(q2_copies)
    q2[...] = added(q1[:, rows64], q2_in, 3).astype(BF16)

    def slot(to):
        return lax.div(to, 2), pl.ds(at128(128 * lax.rem(to, 2)), 128)

    q3_copies = []
    for o in zs:
        k, part = slot(ring(z, o, NZ))
        q3_copies.append(net.put(q2.at[k, :, part], q3_in.at[o - 1], peer(dz=o)))
    landed(s3_copies)
    s3[...] = added(s2[:, pl.ds(at16(16 * x), 16)], s3_in, 3).astype(BF16)
    s4_copies = []
    for o in zs:
        k, part = slot(ring(z, o, NZ))
        s4_copies.append(net.put(s3.at[k, :, part], s4_in.at[o - 1], peer(dz=o)))
    landed(r2_copies)
    r2[...] = added(r1[pl.ds(y, 1)][0], r2_in, 3).astype(BF16)
    r3_copies = [net.put(r2.at[pl.ds(at16(64 * ring(x, o, NX)), 64)], r3_in.at[o - 1], peer(dx=o)) for o in xs]
    spot = 4 * y + x
    own, part = slot(z)
    landed(q3_copies)
    qg[pl.ds(spot, 1)] = added(q2[pl.ds(own, 1), :, part][0], q3_in, NZ - 1).astype(BF16)[None]
    qg_copies = [net.put(qg.at[spot], qg.at[spot], peer(dx=dx, dy=dy)) for dx, dy in xy]
    landed(s4_copies)
    sg[pl.ds(spot, 1)] = added(s3[pl.ds(own, 1), :, part][0], s4_in, NZ - 1).astype(BF16)[None]
    sg_copies = [net.put(sg.at[spot], sg.at[spot], peer(dx=dx, dy=dy)) for dx, dy in xy]

    gain_rows = ugain[:, pl.ds(at128(512 * y + 128 * x), 128)]
    loads[5].wait()
    landed(posx_copies)
    positions = (posx[...].astype(F32).reshape(1024, 128) * gain_rows).astype(BF16)
    embeds = (ce[0, pl.ds(y, 1), :, pl.ds(at128(128 * x), 128)][0].astype(F32) * gain_rows).astype(BF16)
    net.drain(mark)
    mark = len(net.all)
    landed(qg_copies)
    tile = tn(positions, qg[...].reshape(1024, 128))
    landed(sg_copies)
    tile = tile + tn(embeds, sg[...].reshape(256, 128))
    wrows = pl.ds(at16(128 * x), 128)

    def zcols(i):
        return pl.ds(at128(512 * lax.div(i, 2) + 256 * c + 128 * lax.rem(i, 2)), 128)

    weight_out[wrows, zcols(z)] = tile.astype(BF16)
    block = weight_out.at[wrows, zcols(z)]
    near = [1, 7, 2, 6, 3, 5, 4]
    weight_z = [net.put(block, block, peer(dz=o)) for o in near]
    weight_x = [[net.put(block, block, peer(dx=o)) for o in xs]]

    back = nt(sg[pl.ds(4 * x, 4)].reshape(64, 128), uweight[:, zcols(z)]) * gain_part
    half = lax.broadcasted_iota(jnp.int32, (64, 512), 1) // 256
    landed(r3_copies)
    r3 = added(r2[rows64], r3_in, 3)
    back = back + jnp.where(half == c, jnp.concatenate([r3, r3], axis=1), 0.0)
    back = back.reshape(16, 4, 512)
    t[...] = jnp.concatenate([back[:, :, :256], back[:, :, 256:]], axis=1).reshape(8, 2, 8, 256)
    t_copies = [net.put(t.at[ring(z, o, NZ)], t_in.at[o - 1], peer(dz=o)) for o in zs]

    for o, copy in zip(near, weight_z):
        copy.wait_recv()
        block = weight_out.at[wrows, zcols(ring(z, -o, NZ))]
        weight_x.append([net.put(block, block, peer(dx=o)) for o in xs])
    landed(t_copies)
    t2[...] = added(t[pl.ds(z, 1)][0], t_in, NZ - 1)
    t2_copy = net.put(t2.at[ring(c, 1, 2)], t2_in, peer(dc=1))
    final = []
    for o, copies in zip([0] + near[:3], weight_x[:4]):
        landed(copies)
        block = weight_out.at[:, zcols(ring(z, -o, NZ))]
        final.append(net.put(block, block, peer(dc=1)))
    net.drain(mark)
    mark = len(net.all) - 4
    t2_copy.wait_recv()
    item[pl.ds(y, 1)] = t2[pl.ds(c, 1)] + t2_in[...][None]
    item_copies = [net.put(item.at[y], item.at[y], peer(dy=o)) for o in ys]
    for o, copies in zip(near[3:], weight_x[4:]):
        landed(copies)
        block = weight_out.at[:, zcols(ring(z, -o, NZ))]
        final.append(net.put(block, block, peer(dc=1)))
    net.drain(mark)
    landed(item_copies)
    for k in range(NY):
        item_out[:, 512 * k:512 * k + 256] = item[k, :4]
        item_out[:, 512 * k + 256:512 * k + 512] = item[k, 4:]
    landed(final)
    net.drain()


def local(
    item_states, item_scores, item_lengths, item_gain, value_weight,
    user_items, negatives, position_embed, user_gain, user_weight,
):
    def vm(*shape, dtype=BF16):
        return pltpu.VMEM(shape, dtype)

    return pl.pallas_call(
        whole_kernel,
        out_shape=(vm(4, HV, dtype=F32), vm(512, HV)),
        in_specs=[ANY] * 10,
        out_specs=(VM, VM),
        scratch_shapes=[
            pltpu.SMEM((4,), jnp.int32), vm(1, 1024, dtype=F32), vm(1, HV, dtype=F32),
            vm(1, 256, dtype=jnp.int32), vm(1, 256, dtype=jnp.int32),
            vm(4, 256, 1024), vm(4, 16, 256, dtype=F32), vm(1024, HV), vm(512, HV), vm(256, HV),
            vm(8, 256, dtype=jnp.int32),
            vm(8, 256, dtype=F32), vm(3, 8, 256, dtype=F32),
            vm(4, 8, 256, dtype=F32), vm(4, 4, 8, 256, dtype=F32), vm(16, 512, dtype=F32),
            vm(4, 16, 128, dtype=F32), vm(3, 16, 128, dtype=F32),
            vm(4, 16, 512), vm(4, 16, 512, dtype=F32), vm(3, 16, 512, dtype=F32),
            vm(4, 256, 128), vm(8, 256, dtype=jnp.int32),
            vm(2, 4, 256, 512), vm(4, 256, 512),
            vm(256, HV, dtype=F32), vm(256, HV, dtype=F32), vm(256, HV, dtype=F32), vm(256, HV),
            vm(256, HV, dtype=F32), vm(256, HV, dtype=F32),
            vm(4, 256, 512), vm(4, 256, 512), vm(4, 256, 512),
            vm(4, 256, 256), vm(4, 256, 256), vm(4, 256, 256),
            vm(4, 256, 256), vm(4, 256, 256), vm(4, 256, 256),
            vm(3, 4, 64, 256), vm(3, 256, 256), vm(3, 4, 64, 256),
            vm(4, 64, 256), vm(256, 256), vm(4, 64, 256),
            vm(3, 4, 16, 256), vm(3, 64, 256), vm(7, 64, 128),
            vm(4, 16, 256), vm(7, 16, 128),
            vm(16, 64, 128), vm(16, 16, 128),
            vm(8, 2, 8, 256, dtype=F32), vm(7, 2, 8, 256, dtype=F32), vm(2, 8, 256, dtype=F32),
            vm(8, 256, dtype=F32), vm(4, 8, 256, dtype=F32),
            pltpu.SemaphoreType.DMA((COPIES,)),
            pltpu.SemaphoreType.DMA((COPIES,)),
            pltpu.SemaphoreType.DMA((12,)),
        ],
        compiler_params=pltpu.CompilerParams(
            collective_id=0, has_side_effects=True, vmem_limit_bytes=60 * 2**20
        ),
        name="whole",
    )(
        item_lengths, item_states, item_scores, item_gain.reshape(1, -1), value_weight,
        position_embed, user_gain.reshape(1, HV), user_weight, user_items, negatives,
    )


def solution(mesh):
    return jax.shard_map(
        local,
        mesh=mesh,
        in_specs=(
            P("dp", None, "fsdp"), P("dp", None, None), P("dp"), P("fsdp"), P("fsdp", None),
            P("dp", "fsdp"), P("dp", None), P("fsdp", None), P(), P("fsdp", None),
        ),
        out_specs=(P("dp", None), P("fsdp", None)),
        check_vma=False,
    )
```

```python
import jax
import jax.numpy as jnp
from jax import lax
from jax.experimental import pallas as pl
from jax.experimental.pallas import tpu as pltpu
from jax.sharding import PartitionSpec as P

MESH = pl.DeviceIdType.MESH
F32, BF16 = jnp.float32, jnp.bfloat16
NX, NY, NZ = 4, 4, 8
D, HV, ULEN, USERS = 4096, 2048, 1024, 64
TILES, CHUNK = 4, 512
VM = pl.BlockSpec(memory_space=pltpu.VMEM)
ANY = pl.BlockSpec(memory_space=pl.ANY)
COPIES = 250


def place():
    d, y = lax.axis_index("dp"), lax.axis_index("fsdp")
    return lax.div(d, 16), y, lax.rem(lax.div(d, 2), 8), lax.rem(d, 2)


class Indices:
    def __init__(self):
        self.known = {}

    def ring(self, i, o, n):
        key = (id(i), o % n, n)
        if key not in self.known:
            ahead = i + o % n
            self.known[key] = (i, jnp.where(ahead >= n, ahead - n, ahead) if o % n else i)
        return self.known[key][1]

    def halves(self, i):
        key = (id(i), 2)
        if key not in self.known:
            half = sum(jnp.where(i >= k, 1, 0) for k in (2, 4, 6))
            self.known[key] = (i, (half, i - 2 * half))
        return self.known[key][1]


def at128(i):
    return pl.multiple_of(i, 128)


def at16(i):
    return pl.multiple_of(i, 16)


def nt(a, b):
    return lax.dot_general(a, b, (((1,), (1,)), ((), ())), preferred_element_type=F32)


def tn(a, b):
    return lax.dot_general(a, b, (((0,), (0,)), ((), ())), preferred_element_type=F32)


def mm(a, b):
    return jnp.dot(a, b, preferred_element_type=F32)


def split(v):
    hi = v.astype(BF16)
    return hi, (v - hi.astype(F32)).astype(BF16)


def greet(peers):
    barrier = pltpu.get_barrier_semaphore()
    for x, y, z, c in peers:
        pl.semaphore_signal(barrier, inc=1, device_id=((x * NZ + z) * 2 + c, y), device_id_type=MESH)
    return barrier, len(peers)


class Net:
    def __init__(self, send, recv):
        self.send, self.recv, self.all, self.sent = send, recv, [], 0

    def put(self, src, dst, where):
        x, y, z, c = where
        k = len(self.all)
        assert k < COPIES
        copy = pltpu.make_async_remote_copy(
            src_ref=src,
            dst_ref=dst,
            send_sem=self.send.at[k],
            recv_sem=self.recv.at[k],
            device_id=((x * NZ + z) * 2 + c, y),
            device_id_type=MESH,
        )
        copy.start()
        self.all.append(copy)
        return copy

    def drain(self, upto=None):
        upto = len(self.all) if upto is None else upto
        for copy in self.all[self.sent:upto]:
            copy.wait_send()
        self.sent = upto


def landed(copies):
    for copy in copies:
        copy.wait_recv()


def added(own, parts, count):
    total = own.astype(F32)
    for k in range(count):
        total = total + parts[k].astype(F32)
    return total


def whole_kernel(
    lengths_h, states_h, scores_h, igain_h, vweight_h, pos_h, ugain_h, uweight_h, ids_h, negs_h,
    item_out, weight_out,
    lengths, igain, ugain, ids, negs, states, scores, vweight, uweight, pos, ids8,
    squares, squares_in, num, num_in, cat, ep, ep_in, pin, pback, pback_in, posx, nxt, ce, pp,
    in_v, ep_v, u_v, uh_v, ug_v,
    s, q, r, s1_in, q1_in, r1_in, s1, q1, r1, s2_in, r2_in, q2_in, s2, r2, q2, s3_in, r3_in, q3_in, s3, s4_in,
    qg, sg, t, t_in, t2, t2_in, item,
    send, recv, local,
):
    x, y, z, c = place()
    indices = Indices()
    ring, halves_of = indices.ring, indices.halves
    pair, low = halves_of(z)
    group = 4 * x + pair
    member, quarter = 2 * low + c, 2 * c + low
    base = z - low
    net = Net(send, recv)

    def peer(dx=0, dy=0, dz=0, dc=0):
        return ring(x, dx, NX), ring(y, dy, NY), ring(z, dz, NZ), ring(c, dc, 2)

    def mate(om, oy):
        m = ring(member, om, 4)
        hi, lo = halves_of(m)
        return x, ring(y, oy, NY), base + hi, lo

    rows16, rows64 = pl.ds(at16(16 * group), 16), pl.ds(at16(64 * x), 64)
    mine, theirs = pl.ds(at128(256 * c), 256), pl.ds(at128(256 * ring(c, 1, 2)), 256)
    own512 = pl.ds(at128(512 * y), 512)
    loads = [
        pltpu.make_async_copy(pos_h.at[rows16, own512], pin.at[0], local.at[0]),
        pltpu.make_async_copy(uweight_h, uweight, local.at[1]),
        pltpu.make_async_copy(scores_h, scores, local.at[2]),
        pltpu.make_async_copy(vweight_h, vweight, local.at[3]),
        pltpu.make_async_copy(pos_h.at[:, pl.ds(at128(512 * y + 128 * x), 128)], posx.at[y], local.at[4]),
        pltpu.make_async_copy(pos_h, pos, local.at[5]),
        pltpu.make_async_copy(lengths_h, lengths, local.at[7]),
        pltpu.make_async_copy(igain_h, igain, local.at[8]),
        pltpu.make_async_copy(ugain_h, ugain, local.at[9]),
        pltpu.make_async_copy(ids_h, ids, local.at[10]),
        pltpu.make_async_copy(negs_h, negs, local.at[11]),
    ]
    item_loads = [pltpu.make_async_copy(states_h.at[i], states.at[i], local.at[12 + i]) for i in range(4)]
    for load in item_loads:
        load.start()
    loads[2].start()
    offsets = [(om, oy) for om in range(4) for oy in range(4) if om or oy]
    zs, xs, ys = (4, 3, 5, 2, 6, 1, 7), range(1, NX), range(1, NY)
    xy = [(dx, dy) for dx in range(NX) for dy in range(NY) if dx or dy]
    barrier, count = greet(
        [mate(om, oy) for om, oy in offsets]
        + [peer(dz=o) for o in zs]
        + [peer(dx=dx, dy=dy) for dx, dy in xy if dx]
    )
    for load in loads[6:]:
        load.start()

    ones = jnp.ones((8, 256), BF16)
    item_row = lax.broadcasted_iota(jnp.int32, (8, 256), 0)
    sums = jnp.zeros((8, 256), F32)
    for i in range(4):
        item_loads[i].wait()
        part = jnp.zeros((256, 128), F32)
        for j in range(8):
            v = states[i, :, 128 * j:128 * (j + 1)].astype(F32)
            part = part + v * v
        sums = jnp.where(item_row == i, nt(ones, jnp.concatenate(split(part), axis=1)), sums)
    for k in (0, 1, 3, 5, 4):
        loads[k].start()
    for load in loads[6:]:
        load.wait()
    ids8[...] = jnp.broadcast_to(ids[...], (8, 256))
    squares[...] = sums
    pl.semaphore_wait(barrier, count)
    square_copies = [net.put(squares, squares_in.at[o - 1], peer(dy=o)) for o in ys]
    pin_copies = [
        net.put(pos_h.at[rows16, pl.ds(at128(512 * ring(y, o, NY)), 512)], pin.at[o], peer(dy=o)) for o in ys
    ]
    next_copy = net.put(ids8, nxt, peer(dy=-1))
    loads[2].wait()
    token = lax.broadcasted_iota(jnp.int32, (16, 256), 1)
    for i in range(4):
        weights = jnp.where(token < lengths[i], jnp.exp(scores[i]), 0.0)
        scores[i] = weights / jnp.sum(weights, axis=1, keepdims=True)

    loads[0].wait()
    loads[1].wait()
    landed(pin_copies)
    gain_part = ugain[:, own512]
    pos_rows = pin[...].astype(F32).reshape(64, 512) * gain_part
    pback[...] = mm(
        pos_rows.astype(BF16), uweight[:, pl.ds(at128(512 * quarter), 512)]
    ).reshape(4, 16, 512)
    back_copies = [net.put(pback.at[o], pback_in.at[o - 1], peer(dy=-o)) for o in ys]

    landed(square_copies)
    inv_rms = lax.rsqrt((squares[...] + squares_in[0] + squares_in[1] + squares_in[2]) / D + 1e-05)
    pooled_hi, pooled_lo = [], []
    for i in range(4):
        hi, lo = split(scores[i] * inv_rms[i:i + 1])
        both = mm(jnp.concatenate([hi, lo], axis=0), states[i])
        pooled = (both[:16] + both[16:]) * igain[...]
        hi, lo = split(pooled)
        pooled_hi.append(hi)
        pooled_lo.append(lo)
    left = jnp.concatenate(pooled_hi + pooled_lo, axis=0)
    loads[3].wait()
    head = lax.broadcasted_iota(jnp.int32, (4, 16, 256), 1)
    tile = lax.broadcasted_iota(jnp.int32, (4, 16, 256), 2) // 128
    for j in range(8):
        full = mm(left, vweight[:, 256 * j:256 * (j + 1)])
        full = (full[:64] + full[64:]).reshape(4, 16, 256)
        block = jnp.sum(jnp.where(head == tile + 2 * j, full, 0.0), axis=1)
        num[j // 2, 4 * (j % 2):4 * (j % 2) + 4, :] = block
    num_copies = []
    for om, oy in offsets:
        num_copies.append(net.put(num.at[ring(y, oy, NY)], num_in.at[oy, member], mate(om, oy)))
    num_in[0, pl.ds(member, 1)] = num[pl.ds(y, 1)]
    mark = len(net.all) - 15

    landed(back_copies)
    pp[pl.ds(quarter, 1), rows16] = (pback[0] + pback_in[0] + pback_in[1] + pback_in[2]).astype(BF16)[None]
    own = pp.at[quarter, rows16]
    pp_z = [net.put(own, own, peer(dz=o)) for o in zs]

    landed(num_copies)
    for m in range(4):
        total = num_in[0, m] + num_in[1, m] + num_in[2, m] + num_in[3, m]
        cat[4 * m:4 * m + 4, :256] = total[:4]
        cat[4 * m:4 * m + 4, 256:] = total[4:]
    embed = cat[...].astype(BF16)
    gained = (embed.astype(F32) * gain_part).astype(BF16)
    for k in range(NY):
        ep[k] = mm(gained, uweight[:, pl.ds(at128(512 * k + 128 * quarter), 128)])
    ep_copies = [net.put(ep.at[ring(y, o, NY)], ep_in.at[o - 1], peer(dy=o)) for o in ys]
    part = pl.ds(at128(128 * quarter), 128)
    ce[0, pl.ds(y, 1), rows16, part] = cat[:, part].astype(BF16)[None]
    block = ce.at[0, y, rows16, part]
    cat_z = [net.put(block, block, peer(dz=o)) for o in zs]

    landed(pp_z)
    own = pp.at[pl.ds(2 * c, 2), rows64]
    pp_x = [net.put(own, own, peer(dx=o)) for o in xs]

    net.drain(mark)
    mark = len(net.all) - 17
    landed(ep_copies)
    ce[1, pl.ds(y, 1), rows16, part] = (ep[pl.ds(y, 1)] + ep_in[0] + ep_in[1] + ep_in[2]).astype(BF16)
    block = ce.at[1, y, rows16, part]
    ep_z = [net.put(block, block, peer(dz=o)) for o in zs]

    halves = [pl.ds(at128(256 * c + 128 * h), 128) for h in range(2)]

    def second(a):
        by_x = [net.put(ce.at[a, y, rows64, halves[0]], ce.at[a, y, rows64, halves[0]], peer(dx=o)) for o in xs]
        by_y = [net.put(ce.at[a, y, rows64, halves[1]], ce.at[a, y, rows64, halves[1]], peer(dy=o)) for o in ys]
        return by_x, by_y

    def third(a, by_x, by_y):
        landed(by_x)
        block = ce.at[a, y, :, halves[0]]
        to_y = [net.put(block, block, peer(dy=o)) for o in ys]
        landed(by_y)
        block = ce.at[a, :, rows64, halves[1]]
        to_x = [net.put(block, block, peer(dx=o)) for o in xs]
        block = ce.at[a, y, :, halves[0]]
        shared = [net.put(block, block, peer(dc=1))]
        block = ce.at[a, :, rows64, halves[1]]
        shared.append(net.put(block, block, peer(dc=1)))
        return to_y, to_x, shared

    def fourth(a, to_y, to_x, shared):
        for o in range(1, 4):
            to_y[o - 1].wait_recv()
            block = ce.at[a, ring(y, -o, NY), :, halves[0]]
            shared.append(net.put(block, block, peer(dc=1)))
            to_x[o - 1].wait_recv()
            block = ce.at[a, :, pl.ds(at16(64 * ring(x, -o, NX)), 64), halves[1]]
            shared.append(net.put(block, block, peer(dc=1)))
        return shared

    net.drain(mark)
    mark = len(net.all)
    landed(cat_z)
    cat_2 = second(0)
    landed(ep_z)
    ep_2 = second(1)
    landed(pp_x)
    own = pp.at[pl.ds(2 * c, 2)]
    pp_final = net.put(own, own, peer(dc=1))
    cat_3 = third(0, *cat_2)
    ep_3 = third(1, *ep_2)
    cat_4 = fourth(0, *cat_3)
    ep_4 = fourth(1, *ep_3)
    posx_copies = [
        net.put(pos_h.at[:, pl.ds(at128(512 * ring(y, o, NY) + 128 * x), 128)], posx.at[y], peer(dy=o)) for o in ys
    ]
    net.drain(mark)
    mark = len(net.all)
    landed(cat_4)
    landed([next_copy])
    loads[5].wait()

    js = [slice(CHUNK * k, CHUNK * (k + 1)) for k in range(TILES)]
    all_items = lax.broadcasted_iota(jnp.int32, (256, 256), 0)
    hot_t32 = (all_items == ids[...]).astype(F32)
    hot_t = hot_t32.astype(BF16)
    hot = hot_t32.T.astype(BF16)
    lane = lax.broadcasted_iota(jnp.int32, (8, 256), 1)
    targets = jnp.where(lane == 255, pltpu.roll(nxt[...], 255, 1), pltpu.roll(ids8[...], 255, 1))[:1]
    target_t = (all_items == targets).astype(F32)
    counts = jnp.sum((all_items == negs[...]).astype(F32), axis=1, keepdims=True)
    spots = y * 256 + lax.broadcasted_iota(jnp.int32, (1, 256), 1)
    scale = jnp.where(spots < ULEN - 1, 1.0 / (USERS * (ULEN - 1)), 0.0)

    in_squares = jnp.zeros((256, 1), F32)
    cat_squares = jnp.zeros((256, 1), F32)
    for k, j in enumerate(js):
        v = mm(hot, ce[0, k]) + pos[:, j].astype(F32)
        in_v[:, j] = v
        in_squares += jnp.sum(v * v, axis=1, keepdims=True)
        w = ce[0, k].astype(F32)
        cat_squares += jnp.sum(w * w, axis=1, keepdims=True)
    inv = lax.rsqrt(in_squares / HV + 1e-05)
    cat_inv = 1.0 / jnp.sqrt(cat_squares + 1e-06)
    landed(ep_4)
    pp_final.wait_recv()
    out_squares = jnp.zeros((256, 1), F32)
    for k, j in enumerate(js):
        e = mm(hot, ce[1, k]) + pp[k].astype(F32)
        ep_v[:, j] = e
        v = in_v[:, j] + inv * e
        u_v[:, j] = v
        out_squares += jnp.sum(v * v, axis=1, keepdims=True)
    out_inv = 1.0 / jnp.sqrt(out_squares + 1e-06)
    logits = jnp.zeros((256, 256), F32)
    for k, j in enumerate(js):
        hi, lo = split(u_v[:, j] * out_inv)
        uh_v[:, j] = hi
        logits += nt(ce[0, k], hi) + nt(ce[0, k], lo)
    logits = 20.0 * cat_inv * logits
    powers = jnp.exp(logits)
    pos_power = jnp.sum(target_t * powers, axis=0, keepdims=True)
    total = pos_power + jnp.sum(counts * powers, axis=0, keepdims=True)
    grad_t = scale * (counts * powers / total + target_t * (pos_power / total - 1.0))
    moved = grad_t * logits
    cat_along = jnp.sum(moved, axis=1, keepdims=True) * cat_inv
    along = jnp.sum(moved.T, axis=1, keepdims=True) * out_inv
    by_row, by_row_lo = split((grad_t * (20.0 * cat_inv)).T)
    inner = jnp.zeros((256, 1), F32)
    s1_copies, q1_copies, r1_copies, s2_copies, q2_copies = [], [], [], [], []

    def chips(k):
        q1_copies[k].wait_recv()
        q1[k] = (q[k, :, mine].astype(F32) + q1_in[k].astype(F32)).astype(BF16)
        for o in xs if k % 2 else ():
            rows = pl.ds(at16(64 * ring(x, o, NX)), 64)
            q2_copies.append(net.put(q1.at[k - 1:k + 1, rows], q2_in.at[o - 1, k - 1:k + 1], peer(dx=o)))
        s1_copies[k].wait_recv()
        s1[k] = (s[k, :, mine].astype(F32) + s1_in[k].astype(F32)).astype(BF16)
        for o in ys if k % 2 else ():
            rows = pl.ds(at16(64 * ring(y, o, NY)), 64)
            s2_copies.append(net.put(s1.at[k - 1:k + 1, rows], s2_in.at[o - 1, k - 1:k + 1], peer(dy=o)))

    for k, j in enumerate(js):
        g = mm(by_row, ce[0, k]) + mm(by_row_lo, ce[0, k])
        g = (g - u_v[:, j] * along) * out_inv
        ug_v[:, j] = g
        rows = (inv * g).astype(BF16)
        q[k] = rows
        q1_copies.append(net.put(q.at[k, :, theirs], q1_in.at[k], peer(dc=1)))
        s[k] = mm(hot_t, rows).astype(BF16)
        s1_copies.append(net.put(s.at[k, :, theirs], s1_in.at[k], peer(dc=1)))
        inner += jnp.sum(g * ep_v[:, j], axis=1, keepdims=True)
        if k:
            chips(k - 1)
    inner = inner * (inv * inv * inv / HV)
    by_item = grad_t.astype(BF16)
    chips(TILES - 1)
    for k, j in enumerate(js):
        direct = (ug_v[:, j] - in_v[:, j] * inner).astype(BF16)
        item_grad = (20.0 * mm(by_item, uh_v[:, j]) - ce[0, k].astype(F32) * cat_along) * cat_inv
        r[k] = (mm(hot_t, direct) + item_grad).astype(BF16)
        r1_copies.append(net.put(r.at[k, :, theirs], r1_in.at[k], peer(dc=1)))
    for k in range(TILES):
        r1_copies[k].wait_recv()
        r1[k] = (r[k, :, mine].astype(F32) + r1_in[k].astype(F32)).astype(BF16)
    r2_copies = [net.put(r1.at[ring(y, o, NY)], r2_in.at[o - 1], peer(dy=o)) for o in ys]

    net.drain(mark)
    mark = len(net.all)
    landed(s2_copies)
    s2[...] = added(s1[:, pl.ds(at16(64 * y), 64)], s2_in, 3).astype(BF16)
    s3_copies = [net.put(s2.at[:, pl.ds(at16(16 * ring(x, o, NX)), 16)], s3_in.at[o - 1], peer(dx=o)) for o in xs]
    landed(q2_copies)
    q2[...] = added(q1[:, rows64], q2_in, 3).astype(BF16)

    def slot(to):
        hi, lo = halves_of(to)
        return hi, pl.ds(at128(128 * lo), 128)

    q3_copies = []
    for o in zs:
        k, part = slot(ring(z, o, NZ))
        q3_copies.append(net.put(q2.at[k, :, part], q3_in.at[o - 1], peer(dz=o)))
    landed(s3_copies)
    s3[...] = added(s2[:, pl.ds(at16(16 * x), 16)], s3_in, 3).astype(BF16)
    s4_copies = []
    for o in zs:
        k, part = slot(ring(z, o, NZ))
        s4_copies.append(net.put(s3.at[k, :, part], s4_in.at[o - 1], peer(dz=o)))
    spot = 4 * y + x
    own, part = slot(z)
    landed(q3_copies)
    qg[pl.ds(spot, 1)] = added(q2[pl.ds(own, 1), :, part][0], q3_in, NZ - 1).astype(BF16)[None]
    qg_copies = [net.put(qg.at[spot], qg.at[spot], peer(dx=dx, dy=dy)) for dx, dy in xy]
    landed(r2_copies)
    r2[...] = added(r1[pl.ds(y, 1)][0], r2_in, 3).astype(BF16)
    r3_copies = [net.put(r2.at[pl.ds(at16(64 * ring(x, o, NX)), 64)], r3_in.at[o - 1], peer(dx=o)) for o in xs]
    landed(s4_copies)
    sg[pl.ds(spot, 1)] = added(s3[pl.ds(own, 1), :, part][0], s4_in, NZ - 1).astype(BF16)[None]
    sg_copies = [net.put(sg.at[spot], sg.at[spot], peer(dx=dx, dy=dy)) for dx, dy in xy]

    gain_rows = ugain[:, pl.ds(at128(512 * y + 128 * x), 128)]
    loads[4].wait()
    landed(posx_copies)
    positions = (posx[...].astype(F32).reshape(1024, 128) * gain_rows).astype(BF16)
    embeds = (ce[0, pl.ds(y, 1), :, pl.ds(at128(128 * x), 128)][0].astype(F32) * gain_rows).astype(BF16)
    net.drain(mark)
    mark = len(net.all)
    landed(qg_copies)
    tile = tn(positions, qg[...].reshape(1024, 128))
    landed(sg_copies)
    tile = tile + tn(embeds, sg[...].reshape(256, 128))
    wrows = pl.ds(at16(128 * x), 128)

    def zcols(i):
        hi, lo = halves_of(i)
        return pl.ds(at128(512 * hi + 256 * c + 128 * lo), 128)

    weight_out[wrows, zcols(z)] = tile.astype(BF16)
    block = weight_out.at[wrows, zcols(z)]
    near = [1, 7, 2, 6, 3, 5, 4]
    weight_z = [net.put(block, block, peer(dz=o)) for o in near]
    weight_x = [[net.put(block, block, peer(dx=o)) for o in xs]]

    back = nt(sg[pl.ds(4 * x, 4)].reshape(64, 128), uweight[:, zcols(z)]) * gain_part
    half = lax.broadcasted_iota(jnp.int32, (64, 512), 1) // 256
    landed(r3_copies)
    r3 = added(r2[rows64], r3_in, 3)
    back = back + jnp.where(half == c, jnp.concatenate([r3, r3], axis=1), 0.0)
    back = back.reshape(16, 4, 512)
    t[...] = jnp.concatenate([back[:, :, :256], back[:, :, 256:]], axis=1).reshape(8, 2, 8, 256)
    t_copies = [net.put(t.at[ring(z, o, NZ)], t_in.at[o - 1], peer(dz=o)) for o in zs]

    for o, copy in zip(near, weight_z):
        copy.wait_recv()
        block = weight_out.at[wrows, zcols(ring(z, -o, NZ))]
        weight_x.append([net.put(block, block, peer(dx=o)) for o in xs])
    landed(t_copies)
    t2[...] = added(t[pl.ds(z, 1)][0], t_in, NZ - 1)
    t2_copy = net.put(t2.at[ring(c, 1, 2)], t2_in, peer(dc=1))
    net.drain(mark)
    mark = len(net.all)
    t2_copy.wait_recv()
    item[pl.ds(y, 1)] = t2[pl.ds(c, 1)] + t2_in[...][None]
    item_copies = [net.put(item.at[y], item.at[y], peer(dy=o)) for o in ys]
    final = []
    for o, copies in zip([0] + near[:3], weight_x[:4]):
        landed(copies)
        block = weight_out.at[:, zcols(ring(z, -o, NZ))]
        final.append(net.put(block, block, peer(dc=1)))
    for o, copies in zip(near[3:], weight_x[4:]):
        landed(copies)
        block = weight_out.at[:, zcols(ring(z, -o, NZ))]
        final.append(net.put(block, block, peer(dc=1)))
    net.drain(mark)
    landed(item_copies)
    for k in range(NY):
        item_out[:, 512 * k:512 * k + 256] = item[k, :4]
        item_out[:, 512 * k + 256:512 * k + 512] = item[k, 4:]
    landed(final)
    net.drain()


def deliver_kernel(item_grads, weight_grad, item_out, weight_out, sems):
    copies = [
        pltpu.make_async_copy(weight_grad, weight_out, sems.at[0]),
        pltpu.make_async_copy(item_grads, item_out, sems.at[1]),
    ]
    for copy in copies:
        copy.start()
    for copy in copies:
        copy.wait()


def local(
    item_states, item_scores, item_lengths, item_gain, value_weight,
    user_items, negatives, position_embed, user_gain, user_weight,
):
    def vm(*shape, dtype=BF16):
        return pltpu.VMEM(shape, dtype)

    item_grads, weight_grad = pl.pallas_call(
        whole_kernel,
        out_shape=(vm(4, HV, dtype=F32), vm(512, HV)),
        in_specs=[ANY] * 10,
        out_specs=(VM, VM),
        scratch_shapes=[
            pltpu.SMEM((4,), jnp.int32), vm(1, 1024, dtype=F32), vm(1, HV, dtype=F32),
            vm(1, 256, dtype=jnp.int32), vm(1, 256, dtype=jnp.int32),
            vm(4, 256, 1024), vm(4, 16, 256, dtype=F32), vm(1024, HV), vm(512, HV), vm(256, HV),
            vm(8, 256, dtype=jnp.int32),
            vm(8, 256, dtype=F32), vm(3, 8, 256, dtype=F32),
            vm(4, 8, 256, dtype=F32), vm(4, 4, 8, 256, dtype=F32), vm(16, 512, dtype=F32),
            vm(4, 16, 128, dtype=F32), vm(3, 16, 128, dtype=F32),
            vm(4, 16, 512), vm(4, 16, 512, dtype=F32), vm(3, 16, 512, dtype=F32),
            vm(4, 256, 128), vm(8, 256, dtype=jnp.int32),
            vm(2, 4, 256, 512), vm(4, 256, 512),
            vm(256, HV, dtype=F32), vm(256, HV, dtype=F32), vm(256, HV, dtype=F32), vm(256, HV),
            vm(256, HV, dtype=F32),
            vm(4, 256, 512), vm(4, 256, 512), vm(4, 256, 512),
            vm(4, 256, 256), vm(4, 256, 256), vm(4, 256, 256),
            vm(4, 256, 256), vm(4, 256, 256), vm(4, 256, 256),
            vm(3, 4, 64, 256), vm(3, 256, 256), vm(3, 4, 64, 256),
            vm(4, 64, 256), vm(256, 256), vm(4, 64, 256),
            vm(3, 4, 16, 256), vm(3, 64, 256), vm(7, 64, 128),
            vm(4, 16, 256), vm(7, 16, 128),
            vm(16, 64, 128), vm(16, 16, 128),
            vm(8, 2, 8, 256, dtype=F32), vm(7, 2, 8, 256, dtype=F32), vm(2, 8, 256, dtype=F32),
            vm(8, 256, dtype=F32), vm(4, 8, 256, dtype=F32),
            pltpu.SemaphoreType.DMA((COPIES,)),
            pltpu.SemaphoreType.DMA((COPIES,)),
            pltpu.SemaphoreType.DMA((16,)),
        ],
        compiler_params=pltpu.CompilerParams(
            collective_id=0, has_side_effects=True, vmem_limit_bytes=60 * 2**20
        ),
        name="whole",
    )(
        item_lengths, item_states, item_scores, item_gain.reshape(1, -1), value_weight,
        position_embed, user_gain.reshape(1, HV), user_weight, user_items, negatives,
    )
    return pl.pallas_call(
        deliver_kernel,
        out_shape=(
            jax.ShapeDtypeStruct((4, HV), F32),
            jax.ShapeDtypeStruct((512, HV), BF16),
        ),
        in_specs=[VM, VM],
        out_specs=(ANY, ANY),
        scratch_shapes=[pltpu.SemaphoreType.DMA((2,))],
        compiler_params=pltpu.CompilerParams(vmem_limit_bytes=8 * 2**20),
        name="deliver",
    )(item_grads, weight_grad)


def solution(mesh):
    return jax.shard_map(
        local,
        mesh=mesh,
        in_specs=(
            P("dp", None, "fsdp"), P("dp", None, None), P("dp"), P("fsdp"), P("fsdp", None),
            P("dp", "fsdp"), P("dp", None), P("fsdp", None), P(), P("fsdp", None),
        ),
        out_specs=(P("dp", None), P("fsdp", None)),
        check_vma=False,
    )
```

```python
import jax
import jax.numpy as jnp
from jax import lax
from jax.experimental import pallas as pl
from jax.experimental.pallas import tpu as pltpu
from jax.sharding import PartitionSpec as P

MESH = pl.DeviceIdType.MESH
F32, BF16 = jnp.float32, jnp.bfloat16
NX, NY, NZ = 4, 4, 8
D, HV, ULEN, USERS = 4096, 2048, 1024, 64
TILES, CHUNK = 4, 512
VM = pl.BlockSpec(memory_space=pltpu.VMEM)
ANY = pl.BlockSpec(memory_space=pl.ANY)
COPIES = 250


def place():
    d, y = lax.axis_index("dp"), lax.axis_index("fsdp")
    return lax.div(d, 16), y, lax.rem(lax.div(d, 2), 8), lax.rem(d, 2)


class Indices:
    def __init__(self):
        self.known = {}

    def ring(self, i, o, n):
        key = (id(i), o % n, n)
        if key not in self.known:
            ahead = i + o % n
            self.known[key] = (i, jnp.where(ahead >= n, ahead - n, ahead) if o % n else i)
        return self.known[key][1]

    def halves(self, i):
        key = (id(i), 2)
        if key not in self.known:
            half = sum(jnp.where(i >= k, 1, 0) for k in (2, 4, 6))
            self.known[key] = (i, (half, i - 2 * half))
        return self.known[key][1]


def at128(i):
    return pl.multiple_of(i, 128)


def at16(i):
    return pl.multiple_of(i, 16)


def nt(a, b):
    return lax.dot_general(a, b, (((1,), (1,)), ((), ())), preferred_element_type=F32)


def tn(a, b):
    return lax.dot_general(a, b, (((0,), (0,)), ((), ())), preferred_element_type=F32)


def mm(a, b):
    return jnp.dot(a, b, preferred_element_type=F32)


def split(v):
    hi = v.astype(BF16)
    return hi, (v - hi.astype(F32)).astype(BF16)


def greet(peers):
    barrier = pltpu.get_barrier_semaphore()
    for x, y, z, c in peers:
        pl.semaphore_signal(barrier, inc=1, device_id=((x * NZ + z) * 2 + c, y), device_id_type=MESH)
    return barrier, len(peers)


class Net:
    def __init__(self, send, recv):
        self.send, self.recv, self.all, self.sent = send, recv, [], 0

    def put(self, src, dst, where):
        x, y, z, c = where
        k = len(self.all)
        assert k < COPIES
        copy = pltpu.make_async_remote_copy(
            src_ref=src,
            dst_ref=dst,
            send_sem=self.send.at[k],
            recv_sem=self.recv.at[k],
            device_id=((x * NZ + z) * 2 + c, y),
            device_id_type=MESH,
        )
        copy.start()
        self.all.append(copy)
        return copy

    def drain(self, upto=None):
        upto = len(self.all) if upto is None else upto
        for copy in self.all[self.sent:upto]:
            copy.wait_send()
        self.sent = upto


def landed(copies):
    for copy in copies:
        copy.wait_recv()


def added(own, parts, count):
    total = own.astype(F32)
    for k in range(count):
        total = total + parts[k].astype(F32)
    return total


def whole_kernel(
    lengths_h, states_h, scores_h, igain_h, vweight_h, pos_h, ugain_h, uweight_h, ids_h, negs_h,
    item_out, weight_out,
    lengths, igain, ugain, ids, negs, states, scores, vweight, uweight, pos, ids8,
    squares, squares_in, num, num_in, cat, ep, ep_in, pin, pback, pback_in, posx, nxt, ce, pp,
    in_v, ep_v, u_v, uh_v, ug_v,
    s, q, r, s1_in, q1_in, r1_in, s1, q1, r1, s2_in, r2_in, q2_in, s2, r2, q2, s3_in, r3_in, q3_in, s3, s4_in,
    qg, sg, t, t_in, t2, t2_in, item,
    send, recv, local,
):
    x, y, z, c = place()
    indices = Indices()
    ring, halves_of = indices.ring, indices.halves
    pair, low = halves_of(z)
    group = 4 * x + pair
    member, quarter = 2 * low + c, 2 * c + low
    base = z - low
    net = Net(send, recv)

    def peer(dx=0, dy=0, dz=0, dc=0):
        return ring(x, dx, NX), ring(y, dy, NY), ring(z, dz, NZ), ring(c, dc, 2)

    def mate(om, oy):
        m = ring(member, om, 4)
        hi, lo = halves_of(m)
        return x, ring(y, oy, NY), base + hi, lo

    rows16, rows64 = pl.ds(at16(16 * group), 16), pl.ds(at16(64 * x), 64)
    mine, theirs = pl.ds(at128(256 * c), 256), pl.ds(at128(256 * ring(c, 1, 2)), 256)
    own512 = pl.ds(at128(512 * y), 512)
    loads = [
        pltpu.make_async_copy(pos_h.at[rows16, own512], pin.at[0], local.at[0]),
        pltpu.make_async_copy(uweight_h, uweight, local.at[1]),
        pltpu.make_async_copy(scores_h, scores, local.at[2]),
        pltpu.make_async_copy(vweight_h, vweight, local.at[3]),
        pltpu.make_async_copy(pos_h.at[:, pl.ds(at128(512 * y + 128 * x), 128)], posx.at[y], local.at[4]),
        pltpu.make_async_copy(pos_h, pos, local.at[5]),
        pltpu.make_async_copy(lengths_h, lengths, local.at[7]),
        pltpu.make_async_copy(igain_h, igain, local.at[8]),
        pltpu.make_async_copy(ugain_h, ugain, local.at[9]),
        pltpu.make_async_copy(ids_h, ids, local.at[10]),
        pltpu.make_async_copy(negs_h, negs, local.at[11]),
    ]
    item_loads = [pltpu.make_async_copy(states_h.at[i], states.at[i], local.at[12 + i]) for i in range(4)]
    for load in item_loads:
        load.start()
    loads[2].start()
    offsets = [(om, oy) for om in range(4) for oy in range(4) if om or oy]
    zs, xs, ys = (4, 3, 5, 2, 6, 1, 7), range(1, NX), range(1, NY)
    xy = [(dx, dy) for dx in range(NX) for dy in range(NY) if dx or dy]
    barrier, count = greet(
        [mate(om, oy) for om, oy in offsets]
        + [peer(dz=o) for o in zs]
        + [peer(dx=dx, dy=dy) for dx, dy in xy if dx]
    )
    for load in loads[6:]:
        load.start()

    ones = jnp.ones((8, 256), BF16)
    item_row = lax.broadcasted_iota(jnp.int32, (8, 256), 0)
    sums = jnp.zeros((8, 256), F32)
    for i in range(4):
        item_loads[i].wait()
        part = jnp.zeros((256, 128), F32)
        for j in range(8):
            v = states[i, :, 128 * j:128 * (j + 1)].astype(F32)
            part = part + v * v
        sums = jnp.where(item_row == i, nt(ones, jnp.concatenate(split(part), axis=1)), sums)
    for k in (0, 1, 3, 5, 4):
        loads[k].start()
    for load in loads[6:]:
        load.wait()
    ids8[...] = jnp.broadcast_to(ids[...], (8, 256))
    squares[...] = sums
    pl.semaphore_wait(barrier, count)
    square_copies = [net.put(squares, squares_in.at[o - 1], peer(dy=o)) for o in ys]
    pin_copies = [
        net.put(pos_h.at[rows16, pl.ds(at128(512 * ring(y, o, NY)), 512)], pin.at[o], peer(dy=o)) for o in ys
    ]
    next_copy = net.put(ids8, nxt, peer(dy=-1))
    loads[2].wait()
    token = lax.broadcasted_iota(jnp.int32, (16, 256), 1)
    for i in range(4):
        weights = jnp.where(token < lengths[i], jnp.exp(scores[i]), 0.0)
        scores[i] = weights / jnp.sum(weights, axis=1, keepdims=True)

    loads[0].wait()
    loads[1].wait()
    landed(pin_copies)
    gain_part = ugain[:, own512]
    pos_rows = pin[...].astype(F32).reshape(64, 512) * gain_part
    pback[...] = mm(
        pos_rows.astype(BF16), uweight[:, pl.ds(at128(512 * quarter), 512)]
    ).reshape(4, 16, 512)
    back_copies = [net.put(pback.at[o], pback_in.at[o - 1], peer(dy=-o)) for o in ys]

    landed(square_copies)
    inv_rms = lax.rsqrt((squares[...] + squares_in[0] + squares_in[1] + squares_in[2]) / D + 1e-05)
    pooled_hi, pooled_lo = [], []
    for i in range(4):
        hi, lo = split(scores[i] * inv_rms[i:i + 1])
        both = mm(jnp.concatenate([hi, lo], axis=0), states[i])
        pooled = (both[:16] + both[16:]) * igain[...]
        hi, lo = split(pooled)
        pooled_hi.append(hi)
        pooled_lo.append(lo)
    left = jnp.concatenate(pooled_hi + pooled_lo, axis=0)
    loads[3].wait()
    head = lax.broadcasted_iota(jnp.int32, (4, 16, 256), 1)
    tile = lax.broadcasted_iota(jnp.int32, (4, 16, 256), 2) // 128
    for j in range(8):
        full = mm(left, vweight[:, 256 * j:256 * (j + 1)])
        full = (full[:64] + full[64:]).reshape(4, 16, 256)
        block = jnp.sum(jnp.where(head == tile + 2 * j, full, 0.0), axis=1)
        num[j // 2, 4 * (j % 2):4 * (j % 2) + 4, :] = block
    num_copies = []
    for om, oy in offsets:
        num_copies.append(net.put(num.at[ring(y, oy, NY)], num_in.at[oy, member], mate(om, oy)))
    num_in[0, pl.ds(member, 1)] = num[pl.ds(y, 1)]
    mark = len(net.all) - 15

    landed(back_copies)
    pp[pl.ds(quarter, 1), rows16] = (pback[0] + pback_in[0] + pback_in[1] + pback_in[2]).astype(BF16)[None]
    own = pp.at[quarter, rows16]
    pp_z = [net.put(own, own, peer(dz=o)) for o in zs]

    landed(num_copies)
    for m in range(4):
        total = num_in[0, m] + num_in[1, m] + num_in[2, m] + num_in[3, m]
        cat[4 * m:4 * m + 4, :256] = total[:4]
        cat[4 * m:4 * m + 4, 256:] = total[4:]
    embed = cat[...].astype(BF16)
    gained = (embed.astype(F32) * gain_part).astype(BF16)
    for k in range(NY):
        ep[k] = mm(gained, uweight[:, pl.ds(at128(512 * k + 128 * quarter), 128)])
    ep_copies = [net.put(ep.at[ring(y, o, NY)], ep_in.at[o - 1], peer(dy=o)) for o in ys]
    part = pl.ds(at128(128 * quarter), 128)
    ce[0, pl.ds(y, 1), rows16, part] = cat[:, part].astype(BF16)[None]
    block = ce.at[0, y, rows16, part]
    cat_z = [net.put(block, block, peer(dz=o)) for o in zs]

    landed(pp_z)
    own = pp.at[pl.ds(2 * c, 2), rows64]
    pp_x = [net.put(own, own, peer(dx=o)) for o in xs]

    net.drain(mark)
    mark = len(net.all) - 17
    landed(ep_copies)
    ce[1, pl.ds(y, 1), rows16, part] = (ep[pl.ds(y, 1)] + ep_in[0] + ep_in[1] + ep_in[2]).astype(BF16)
    block = ce.at[1, y, rows16, part]
    ep_z = [net.put(block, block, peer(dz=o)) for o in zs]

    halves = [pl.ds(at128(256 * c + 128 * h), 128) for h in range(2)]

    def second(a):
        by_x = [net.put(ce.at[a, y, rows64, halves[0]], ce.at[a, y, rows64, halves[0]], peer(dx=o)) for o in xs]
        by_y = [net.put(ce.at[a, y, rows64, halves[1]], ce.at[a, y, rows64, halves[1]], peer(dy=o)) for o in ys]
        return by_x, by_y

    def third(a, by_x, by_y):
        landed(by_x)
        block = ce.at[a, y, :, halves[0]]
        to_y = [net.put(block, block, peer(dy=o)) for o in ys]
        landed(by_y)
        block = ce.at[a, :, rows64, halves[1]]
        to_x = [net.put(block, block, peer(dx=o)) for o in xs]
        block = ce.at[a, y, :, halves[0]]
        shared = [net.put(block, block, peer(dc=1))]
        block = ce.at[a, :, rows64, halves[1]]
        shared.append(net.put(block, block, peer(dc=1)))
        return to_y, to_x, shared

    def fourth(a, to_y, to_x, shared):
        for o in range(1, 4):
            to_y[o - 1].wait_recv()
            block = ce.at[a, ring(y, -o, NY), :, halves[0]]
            shared.append(net.put(block, block, peer(dc=1)))
            to_x[o - 1].wait_recv()
            block = ce.at[a, :, pl.ds(at16(64 * ring(x, -o, NX)), 64), halves[1]]
            shared.append(net.put(block, block, peer(dc=1)))
        return shared

    net.drain(mark)
    mark = len(net.all)
    landed(cat_z)
    cat_2 = second(0)
    landed(ep_z)
    ep_2 = second(1)
    landed(pp_x)
    own = pp.at[pl.ds(2 * c, 2)]
    pp_final = net.put(own, own, peer(dc=1))
    cat_3 = third(0, *cat_2)
    ep_3 = third(1, *ep_2)
    cat_4 = fourth(0, *cat_3)
    ep_4 = fourth(1, *ep_3)
    posx_copies = [
        net.put(pos_h.at[:, pl.ds(at128(512 * ring(y, o, NY) + 128 * x), 128)], posx.at[y], peer(dy=o)) for o in ys
    ]
    net.drain(mark)
    mark = len(net.all)
    landed(cat_4)
    landed([next_copy])
    loads[5].wait()

    js = [slice(CHUNK * k, CHUNK * (k + 1)) for k in range(TILES)]
    all_items = lax.broadcasted_iota(jnp.int32, (256, 256), 0)
    hot_t32 = (all_items == ids[...]).astype(F32)
    hot_t = hot_t32.astype(BF16)
    hot = hot_t32.T.astype(BF16)
    lane = lax.broadcasted_iota(jnp.int32, (8, 256), 1)
    targets = jnp.where(lane == 255, pltpu.roll(nxt[...], 255, 1), pltpu.roll(ids8[...], 255, 1))[:1]
    target_t = (all_items == targets).astype(F32)
    counts = jnp.sum((all_items == negs[...]).astype(F32), axis=1, keepdims=True)
    spots = y * 256 + lax.broadcasted_iota(jnp.int32, (1, 256), 1)
    scale = jnp.where(spots < ULEN - 1, 1.0 / (USERS * (ULEN - 1)), 0.0)

    in_squares = jnp.zeros((256, 1), F32)
    cat_squares = jnp.zeros((256, 1), F32)
    for k, j in enumerate(js):
        v = mm(hot, ce[0, k]) + pos[:, j].astype(F32)
        in_v[:, j] = v
        in_squares += jnp.sum(v * v, axis=1, keepdims=True)
        w = ce[0, k].astype(F32)
        cat_squares += jnp.sum(w * w, axis=1, keepdims=True)
    inv = lax.rsqrt(in_squares / HV + 1e-05)
    cat_inv = 1.0 / jnp.sqrt(cat_squares + 1e-06)
    landed(ep_4)
    pp_final.wait_recv()
    out_squares = jnp.zeros((256, 1), F32)
    for k, j in enumerate(js):
        e = mm(hot, ce[1, k]) + pp[k].astype(F32)
        ep_v[:, j] = e
        v = in_v[:, j] + inv * e
        u_v[:, j] = v
        out_squares += jnp.sum(v * v, axis=1, keepdims=True)
    out_inv = 1.0 / jnp.sqrt(out_squares + 1e-06)
    logits = jnp.zeros((256, 256), F32)
    for k, j in enumerate(js):
        hi, lo = split(u_v[:, j] * out_inv)
        uh_v[:, j] = hi
        logits += nt(ce[0, k], hi) + nt(ce[0, k], lo)
    logits = 20.0 * cat_inv * logits
    powers = jnp.exp(logits)
    pos_power = jnp.sum(target_t * powers, axis=0, keepdims=True)
    total = pos_power + jnp.sum(counts * powers, axis=0, keepdims=True)
    grad_t = scale * (counts * powers / total + target_t * (pos_power / total - 1.0))
    moved = grad_t * logits
    cat_along = jnp.sum(moved, axis=1, keepdims=True) * cat_inv
    along = jnp.sum(moved.T, axis=1, keepdims=True) * out_inv
    by_row = (grad_t * (20.0 * cat_inv)).T.astype(BF16)
    inner = jnp.zeros((256, 1), F32)
    s1_copies, q1_copies, r1_copies, s2_copies, q2_copies = [], [], [], [], []

    def chips(k):
        q1_copies[k].wait_recv()
        q1[k] = (q[k, :, mine].astype(F32) + q1_in[k].astype(F32)).astype(BF16)
        for o in xs if k % 2 else ():
            rows = pl.ds(at16(64 * ring(x, o, NX)), 64)
            q2_copies.append(net.put(q1.at[k - 1:k + 1, rows], q2_in.at[o - 1, k - 1:k + 1], peer(dx=o)))
        s1_copies[k].wait_recv()
        s1[k] = (s[k, :, mine].astype(F32) + s1_in[k].astype(F32)).astype(BF16)
        for o in ys if k % 2 else ():
            rows = pl.ds(at16(64 * ring(y, o, NY)), 64)
            s2_copies.append(net.put(s1.at[k - 1:k + 1, rows], s2_in.at[o - 1, k - 1:k + 1], peer(dy=o)))

    for k, j in enumerate(js):
        g = mm(by_row, ce[0, k])
        g = (g - u_v[:, j] * along) * out_inv
        ug_v[:, j] = g
        rows = (inv * g).astype(BF16)
        q[k] = rows
        q1_copies.append(net.put(q.at[k, :, theirs], q1_in.at[k], peer(dc=1)))
        s[k] = mm(hot_t, rows).astype(BF16)
        s1_copies.append(net.put(s.at[k, :, theirs], s1_in.at[k], peer(dc=1)))
        inner += jnp.sum(g * ep_v[:, j], axis=1, keepdims=True)
        if k:
            chips(k - 1)
    inner = inner * (inv * inv * inv / HV)
    by_item = grad_t.astype(BF16)
    chips(TILES - 1)
    for k, j in enumerate(js):
        direct = (ug_v[:, j] - in_v[:, j] * inner).astype(BF16)
        item_grad = (20.0 * mm(by_item, uh_v[:, j]) - ce[0, k].astype(F32) * cat_along) * cat_inv
        r[k] = (mm(hot_t, direct) + item_grad).astype(BF16)
        r1_copies.append(net.put(r.at[k, :, theirs], r1_in.at[k], peer(dc=1)))
    for k in range(TILES):
        r1_copies[k].wait_recv()
        r1[k] = (r[k, :, mine].astype(F32) + r1_in[k].astype(F32)).astype(BF16)
    r2_copies = [net.put(r1.at[ring(y, o, NY)], r2_in.at[o - 1], peer(dy=o)) for o in ys]

    net.drain(mark)
    mark = len(net.all)
    landed(s2_copies)
    s2[...] = added(s1[:, pl.ds(at16(64 * y), 64)], s2_in, 3).astype(BF16)
    s3_copies = [net.put(s2.at[:, pl.ds(at16(16 * ring(x, o, NX)), 16)], s3_in.at[o - 1], peer(dx=o)) for o in xs]
    landed(q2_copies)
    q2[...] = added(q1[:, rows64], q2_in, 3).astype(BF16)

    def slot(to):
        hi, lo = halves_of(to)
        return hi, pl.ds(at128(128 * lo), 128)

    q3_copies = []
    for o in zs:
        k, part = slot(ring(z, o, NZ))
        q3_copies.append(net.put(q2.at[k, :, part], q3_in.at[o - 1], peer(dz=o)))
    landed(s3_copies)
    s3[...] = added(s2[:, pl.ds(at16(16 * x), 16)], s3_in, 3).astype(BF16)
    s4_copies = []
    for o in zs:
        k, part = slot(ring(z, o, NZ))
        s4_copies.append(net.put(s3.at[k, :, part], s4_in.at[o - 1], peer(dz=o)))
    spot = 4 * y + x
    own, part = slot(z)
    landed(q3_copies)
    qg[pl.ds(spot, 1)] = added(q2[pl.ds(own, 1), :, part][0], q3_in, NZ - 1).astype(BF16)[None]
    qg_copies = [net.put(qg.at[spot], qg.at[spot], peer(dx=dx, dy=dy)) for dx, dy in xy]
    landed(r2_copies)
    r2[...] = added(r1[pl.ds(y, 1)][0], r2_in, 3).astype(BF16)
    r3_copies = [net.put(r2.at[pl.ds(at16(64 * ring(x, o, NX)), 64)], r3_in.at[o - 1], peer(dx=o)) for o in xs]
    landed(s4_copies)
    sg[pl.ds(spot, 1)] = added(s3[pl.ds(own, 1), :, part][0], s4_in, NZ - 1).astype(BF16)[None]
    sg_copies = [net.put(sg.at[spot], sg.at[spot], peer(dx=dx, dy=dy)) for dx, dy in xy]

    gain_rows = ugain[:, pl.ds(at128(512 * y + 128 * x), 128)]
    loads[4].wait()
    landed(posx_copies)
    positions = (posx[...].astype(F32).reshape(1024, 128) * gain_rows).astype(BF16)
    embeds = (ce[0, pl.ds(y, 1), :, pl.ds(at128(128 * x), 128)][0].astype(F32) * gain_rows).astype(BF16)
    net.drain(mark)
    mark = len(net.all)
    landed(qg_copies)
    tile = tn(positions, qg[...].reshape(1024, 128))
    landed(sg_copies)
    tile = tile + tn(embeds, sg[...].reshape(256, 128))
    wrows = pl.ds(at16(128 * x), 128)

    def zcols(i):
        hi, lo = halves_of(i)
        return pl.ds(at128(512 * hi + 256 * c + 128 * lo), 128)

    weight_out[wrows, zcols(z)] = tile.astype(BF16)
    block = weight_out.at[wrows, zcols(z)]
    near = [1, 7, 2, 6, 3, 5, 4]
    weight_z = [net.put(block, block, peer(dz=o)) for o in near]
    weight_x = [[net.put(block, block, peer(dx=o)) for o in xs]]

    back = nt(sg[pl.ds(4 * x, 4)].reshape(64, 128), uweight[:, zcols(z)]) * gain_part
    half = lax.broadcasted_iota(jnp.int32, (64, 512), 1) // 256
    landed(r3_copies)
    r3 = added(r2[rows64], r3_in, 3)
    back = back + jnp.where(half == c, jnp.concatenate([r3, r3], axis=1), 0.0)
    back = back.reshape(16, 4, 512)
    t[...] = jnp.concatenate([back[:, :, :256], back[:, :, 256:]], axis=1).reshape(8, 2, 8, 256)
    t_copies = [net.put(t.at[ring(z, o, NZ)], t_in.at[o - 1], peer(dz=o)) for o in zs]

    for o, copy in zip(near, weight_z):
        copy.wait_recv()
        block = weight_out.at[wrows, zcols(ring(z, -o, NZ))]
        weight_x.append([net.put(block, block, peer(dx=o)) for o in xs])
    landed(t_copies)
    t2[...] = added(t[pl.ds(z, 1)][0], t_in, NZ - 1)
    t2_copy = net.put(t2.at[ring(c, 1, 2)], t2_in, peer(dc=1))
    net.drain(mark)
    mark = len(net.all)
    t2_copy.wait_recv()
    item[pl.ds(y, 1)] = t2[pl.ds(c, 1)] + t2_in[...][None]
    item_copies = [net.put(item.at[y], item.at[y], peer(dy=o)) for o in ys]
    final = []
    for o, copies in zip([0] + near[:3], weight_x[:4]):
        landed(copies)
        block = weight_out.at[:, zcols(ring(z, -o, NZ))]
        final.append(net.put(block, block, peer(dc=1)))
    for o, copies in zip(near[3:], weight_x[4:]):
        landed(copies)
        block = weight_out.at[:, zcols(ring(z, -o, NZ))]
        final.append(net.put(block, block, peer(dc=1)))
    net.drain(mark)
    landed(item_copies)
    for k in range(NY):
        item_out[:, 512 * k:512 * k + 256] = item[k, :4]
        item_out[:, 512 * k + 256:512 * k + 512] = item[k, 4:]
    landed(final)
    net.drain()


def deliver_kernel(item_grads, weight_grad, item_out, weight_out, sems):
    copies = [
        pltpu.make_async_copy(weight_grad, weight_out, sems.at[0]),
        pltpu.make_async_copy(item_grads, item_out, sems.at[1]),
    ]
    for copy in copies:
        copy.start()
    for copy in copies:
        copy.wait()


def local(
    item_states, item_scores, item_lengths, item_gain, value_weight,
    user_items, negatives, position_embed, user_gain, user_weight,
):
    def vm(*shape, dtype=BF16):
        return pltpu.VMEM(shape, dtype)

    item_grads, weight_grad = pl.pallas_call(
        whole_kernel,
        out_shape=(vm(4, HV, dtype=F32), vm(512, HV)),
        in_specs=[ANY] * 10,
        out_specs=(VM, VM),
        scratch_shapes=[
            pltpu.SMEM((4,), jnp.int32), vm(1, 1024, dtype=F32), vm(1, HV, dtype=F32),
            vm(1, 256, dtype=jnp.int32), vm(1, 256, dtype=jnp.int32),
            vm(4, 256, 1024), vm(4, 16, 256, dtype=F32), vm(1024, HV), vm(512, HV), vm(256, HV),
            vm(8, 256, dtype=jnp.int32),
            vm(8, 256, dtype=F32), vm(3, 8, 256, dtype=F32),
            vm(4, 8, 256, dtype=F32), vm(4, 4, 8, 256, dtype=F32), vm(16, 512, dtype=F32),
            vm(4, 16, 128, dtype=F32), vm(3, 16, 128, dtype=F32),
            vm(4, 16, 512), vm(4, 16, 512, dtype=F32), vm(3, 16, 512, dtype=F32),
            vm(4, 256, 128), vm(8, 256, dtype=jnp.int32),
            vm(2, 4, 256, 512), vm(4, 256, 512),
            vm(256, HV, dtype=F32), vm(256, HV, dtype=F32), vm(256, HV, dtype=F32), vm(256, HV),
            vm(256, HV, dtype=F32),
            vm(4, 256, 512), vm(4, 256, 512), vm(4, 256, 512),
            vm(4, 256, 256), vm(4, 256, 256), vm(4, 256, 256),
            vm(4, 256, 256), vm(4, 256, 256), vm(4, 256, 256),
            vm(3, 4, 64, 256), vm(3, 256, 256), vm(3, 4, 64, 256),
            vm(4, 64, 256), vm(256, 256), vm(4, 64, 256),
            vm(3, 4, 16, 256), vm(3, 64, 256), vm(7, 64, 128),
            vm(4, 16, 256), vm(7, 16, 128),
            vm(16, 64, 128), vm(16, 16, 128),
            vm(8, 2, 8, 256, dtype=F32), vm(7, 2, 8, 256, dtype=F32), vm(2, 8, 256, dtype=F32),
            vm(8, 256, dtype=F32), vm(4, 8, 256, dtype=F32),
            pltpu.SemaphoreType.DMA((COPIES,)),
            pltpu.SemaphoreType.DMA((COPIES,)),
            pltpu.SemaphoreType.DMA((16,)),
        ],
        compiler_params=pltpu.CompilerParams(
            collective_id=0, has_side_effects=True, vmem_limit_bytes=60 * 2**20
        ),
        name="whole",
    )(
        item_lengths, item_states, item_scores, item_gain.reshape(1, -1), value_weight,
        position_embed, user_gain.reshape(1, HV), user_weight, user_items, negatives,
    )
    return pl.pallas_call(
        deliver_kernel,
        out_shape=(
            jax.ShapeDtypeStruct((4, HV), F32),
            jax.ShapeDtypeStruct((512, HV), BF16),
        ),
        in_specs=[VM, VM],
        out_specs=(ANY, ANY),
        scratch_shapes=[pltpu.SemaphoreType.DMA((2,))],
        compiler_params=pltpu.CompilerParams(vmem_limit_bytes=8 * 2**20),
        name="deliver",
    )(item_grads, weight_grad)


def solution(mesh):
    return jax.shard_map(
        local,
        mesh=mesh,
        in_specs=(
            P("dp", None, "fsdp"), P("dp", None, None), P("dp"), P("fsdp"), P("fsdp", None),
            P("dp", "fsdp"), P("dp", None), P("fsdp", None), P(), P("fsdp", None),
        ),
        out_specs=(P("dp", None), P("fsdp", None)),
        check_vma=False,
    )
```
